512 devices in a mesh: dp: 16 (over z, y_hi), seq: 32 (over y_lo, x, core).
Axes of the slice: x: 4, y: 8 (y_hi: 2, y_lo: 4; y = y_hi * 4 + y_lo), z: 8, core: 2. Of those that a mesh axis runs over, the one named last changes fastest.
Arguments:
- latents: bfloat16 [16, 32, 256, 3072], P('dp', 'seq'), may hold values from -6 to 6
- cotangent: bfloat16 [16, 32, 256, 3072], P('dp', 'seq'), may hold values from -6 to 6
- weights: bfloat16 [3072, 512], P('seq'), may hold values from -0.109375 to 0.109375
Outputs:
- grad_weights: float32 [3072, 512], P('seq')
The draws below stay inside these ranges and needn't reach their ends.
All inputs are finite; a program needn't handle non-finite values.
Results may differ from the reference program's by a relative error of at most 0.035.
Values may be sent and summed in bfloat16 or wider, within the bound.
No kernel may reach another device: no remote copies, remote signals or barrier semaphores. Data moves between devices by JAX's collectives and lax.ppermute only.
A program may use at most 64 MiB of HBM per device.

```python
import jax
import jax.numpy as jnp
from jax import lax

D = 3072
HD = 128
PATCHES = 256
FRAMES = 32
CLIPS = 16
N_SEQ = 32


def shard_levels(rng, dims, pieces, low, largest):
    loudness, own = 1.0, jax.random.fold_in(rng, 6)
    for position, shards_of in pieces:
        draws = jnp.exp(jax.random.uniform(jax.random.fold_in(own, position), (shards_of,), jnp.float32, low / len(pieces), largest / len(pieces)))
        loudness = loudness * jnp.repeat(draws, dims[position] // shards_of).reshape([-1 if axis == position else 1 for axis in range(len(dims))])
    return loudness


def gaussian(stream_key, dims, scale, bound, shards=(), dtype=jnp.bfloat16):
    gain = shard_levels(stream_key, dims, shards, -0.22, 0.18) if shards else 1.0
    result = jax.random.normal(stream_key, dims, jnp.float32) * scale * gain
    return jnp.minimum(jnp.maximum(result, -bound), bound).astype(dtype)


def setup_inputs(seed: int = 0) -> dict:
    seeds = jax.random.split(jax.random.key(seed), 4)
    return {
        "latents": gaussian(seeds[0], (CLIPS, FRAMES, PATCHES, D), 1.0, 6.0, ((0, 16), (1, 32))),
        "cotangent": gaussian(seeds[1], (CLIPS, FRAMES, PATCHES, D), 1.0, 6.0, ((0, 16), (1, 32))),
        "weights": gaussian(seeds[2], (D, 4 * HD), D ** -0.5, 0.109375, ((0, 32),)),
    }


def normalize(rows):
    wide = rows.astype(jnp.float32)
    mean_square = lax.optimization_barrier(jnp.mean(wide * wide, axis=-1, keepdims=True))
    return (wide * lax.rsqrt(mean_square + 1e-06)).astype(jnp.bfloat16)

def attend(query, keys, values, grad_out):
    head = query.shape[-1]
    scale = 1.0 / head ** 0.5
    qf = query.astype(jnp.float32)
    kf = keys.astype(jnp.float32)
    vf = values.astype(jnp.float32)
    gf = grad_out.astype(jnp.float32)
    scores = jnp.einsum('fpd,gpd->pfg', qf, kf) * scale
    probs = jax.nn.softmax(scores, axis=-1)
    probs_b = probs.astype(jnp.bfloat16).astype(jnp.float32)
    out = jnp.einsum('pfg,gpd->fpd', probs_b, vf).astype(jnp.bfloat16)
    grad_v = jnp.einsum('pfg,fpd->gpd', probs_b, gf).astype(jnp.bfloat16)
    grad_probs = jnp.einsum('fpd,gpd->pfg', gf, vf)
    delta = lax.optimization_barrier(jnp.sum(gf * out.astype(jnp.float32), axis=-1))
    grad_scores = (probs * (grad_probs - jnp.transpose(delta)[:, :, None])).astype(jnp.bfloat16).astype(jnp.float32)
    grad_q = (jnp.einsum('pfg,gpd->fpd', grad_scores, kf) * scale).astype(jnp.bfloat16)
    grad_k = (jnp.einsum('pfg,fpd->gpd', grad_scores, qf) * scale).astype(jnp.bfloat16)
    return (out, grad_q, grad_k, grad_v)

def one_clip(latent, cotan, weights):
    head = weights.shape[1] // 4
    width = latent.shape[-1]
    frames, patches = (latent.shape[0], latent.shape[1])
    normed = normalize(latent.reshape(-1, width))
    tangent = cotan.reshape(-1, width)
    qkv = jnp.dot(normed, weights[:, :3 * head], preferred_element_type=jnp.float32).astype(jnp.bfloat16)
    grad_out = jnp.dot(tangent, weights[:, 3 * head:], preferred_element_type=jnp.float32).astype(jnp.bfloat16)
    qkv = qkv.reshape(frames, patches, 3 * head)
    grad_out = grad_out.reshape(frames, patches, head)
    out, grad_q, grad_k, grad_v = attend(qkv[..., :head], qkv[..., head:2 * head], qkv[..., 2 * head:], grad_out)
    grads = jnp.concatenate([grad_q, grad_k, grad_v], axis=-1).reshape(N_SEQ, -1, 3 * head).astype(jnp.float32)
    outs = out.reshape(N_SEQ, -1, head).astype(jnp.float32)
    normed_g = normed.reshape(N_SEQ, -1, width).astype(jnp.float32)
    tangent_g = tangent.reshape(N_SEQ, -1, width).astype(jnp.float32)
    first = jnp.einsum('nti,ntj->nij', normed_g, grads)
    second = jnp.einsum('nti,ntj->nij', tangent_g, outs)
    partial_value = jnp.concatenate([first, second], axis=-1).astype(jnp.bfloat16).astype(jnp.float32)
    return lax.optimization_barrier(jnp.sum(partial_value, axis=0))

def reference(latents, cotangent, weights):

    def step(total, pair):
        return (total + one_clip(pair[0], pair[1], weights), None)
    start = jnp.zeros(weights.shape, jnp.float32)
    total, _ = lax.scan(step, start, (latents, cotangent))
    return total
```

```python
import itertools

import jax
import jax.numpy as jnp
from jax import lax
from jax.experimental import pallas as pl
from jax.experimental.pallas import tpu as pltpu
from jax.sharding import Mesh
from jax.sharding import PartitionSpec as P

NZ, NYH, NYL, NX, NC = 8, 2, 4, 4, 2
AXES = ("z", "yh", "yl", "x", "c")
BF = jnp.bfloat16
F32 = jnp.float32
VMEM = pl.BlockSpec(memory_space=pltpu.VMEM)
ANY = pl.BlockSpec(memory_space=pl.ANY)


def device(z, yh, yl, x, c):
    return (((z * NYH + yh) * NYL + yl) * NX + x) * NC + c


def everyone():
    return itertools.product(range(NZ), range(NYH), range(NYL), range(NX), range(NC))


def groups(key, order):
    found = {}
    for at in everyone():
        found.setdefault(key(*at), []).append((order(*at), device(*at)))
    return [[d for _, d in sorted(members)] for members in found.values()]


LIGHT = groups(
    lambda z, yh, yl, x, c: (c, z, yh, yl if c else x),
    lambda z, yh, yl, x, c: x if c else yl,
)
SPREAD = groups(
    lambda z, yh, yl, x, c: (c, yh, yl if c else x),
    lambda z, yh, yl, x, c: (x if c else yl, z),
)


def heavy_pairs(step):
    pairs = []
    for z, yh, yl, x, c in everyone():
        y = (yh * NYL + yl + step) % (NYH * NYL)
        to = (z, y // NYL, y % NYL, x, c) if c else (z, yh, yl, (x + step) % NX, c)
        pairs.append((device(z, yh, yl, x, c), device(*to)))
    return pairs


def send(v, step):
    return lax.ppermute(v, AXES, heavy_pairs(step))


def other_core(v):
    return lax.ppermute(v, "c", [(0, 1), (1, 0)])


def exchange(v, members):
    return lax.all_to_all(v, AXES, split_axis=0, concat_axis=0, axis_index_groups=members, tiled=True)


def project_kernel(mine, other, lat, cot, packed, scale, w, sems):
    x, yl, c = lax.axis_index("x"), lax.axis_index("yl"), lax.axis_index("c")
    rows = mine.shape[1]
    copies = []
    for a, b in itertools.product(range(NYL), range(NX)):
        even = lax.rem(b - x + NX, NX) * NYL + a
        odd = lax.rem(a - yl + NYL, NYL) * NX + b
        own, theirs = jnp.where(c == 0, even, odd), jnp.where(c == 0, odd, even)
        base = (a * NX + b) * NC * rows
        for src, index, parity, sem in ((mine, own, c, 0), (other, theirs, 1 - c, 1)):
            at = pl.multiple_of(base + parity * rows, 16)
            copies.append(
                pltpu.make_async_copy(src.at[index], w.at[pl.ds(at, rows)], sems.at[sem, a * NX + b])
            )
    for copy in copies:
        copy.start()
    wide = lat[...].astype(F32)
    r = lax.rsqrt(jnp.mean(wide * wide, axis=-1, keepdims=True) + 1e-06)
    scale[...] = jnp.broadcast_to(r, scale.shape)
    for copy in copies:
        copy.wait()
    head = w.shape[1] // 4
    qkv = jnp.dot(lat[...], w[:, : 3 * head], preferred_element_type=F32) * r
    packed[:, : 3 * head] = qkv.astype(BF)
    packed[:, 3 * head :] = jnp.dot(cot[...], w[:, 3 * head :], preferred_element_type=F32).astype(BF)


def project(mine, other, lat, cot):
    tokens, width = lat.shape
    columns = mine.shape[-1]
    return pl.pallas_call(
        project_kernel,
        out_shape=(
            jax.ShapeDtypeStruct((tokens, columns), BF),
            jax.ShapeDtypeStruct((tokens, 128), F32),
        ),
        in_specs=[ANY, ANY, VMEM, VMEM],
        out_specs=(VMEM, VMEM),
        scratch_shapes=[pltpu.VMEM((width, columns), BF), pltpu.SemaphoreType.DMA((2, NYL * NX))],
        compiler_params=pltpu.CompilerParams(vmem_limit_bytes=24 * 2**20),
        name="project",
    )(mine, other, lat, cot)


def weight_kernel(back, scale, lat, cot, mine, other):
    c = lax.axis_index("c")
    head = back.shape[1] // 4
    rows = mine.shape[1]
    outs = back[:, :head]
    r = jnp.concatenate([scale[...]] * 3, axis=-1)
    grads = (back[:, head:].astype(F32) * r).astype(BF)
    contract = (((0,), (0,)), ((), ()))
    wide = NX * NC * rows
    for a in range(NYL):
        part = slice(a * wide, (a + 1) * wide)
        first = lax.dot_general(lat[:, part], grads, contract, preferred_element_type=F32)
        second = lax.dot_general(cot[:, part], outs, contract, preferred_element_type=F32)
        for b in range(NX):
            even = slice(2 * b * rows, (2 * b + 1) * rows)
            odd = slice((2 * b + 1) * rows, (2 * b + 2) * rows)
            for value, at in ((first, slice(0, 3 * head)), (second, slice(3 * head, 4 * head))):
                mine[a * NX + b, :, at] = jnp.where(c == 0, value[even], value[odd]).astype(BF)
                other[a * NX + b, :, at] = jnp.where(c == 0, value[odd], value[even]).astype(BF)


def weight_parts(back, scale, lat, cot):
    width, columns = lat.shape[1], back.shape[1]
    rows = width // (NYL * NX * NC)
    shape = jax.ShapeDtypeStruct((NYL * NX, rows, columns), BF)
    return pl.pallas_call(
        weight_kernel,
        out_shape=(shape, shape),
        in_specs=[VMEM] * 4,
        out_specs=(VMEM, VMEM),
        compiler_params=pltpu.CompilerParams(vmem_limit_bytes=32 * 2**20),
        name="weight_parts",
    )(back, scale, lat, cot)


def split_kernel(mine, arrived, own, plus, minus, two_a, two_b):
    x, yl, c = lax.axis_index("x"), lax.axis_index("yl"), lax.axis_index("c")

    def total(offset, t):
        even = t * NX + lax.rem(x + offset, NX)
        odd = lax.rem(yl + offset, NYL) * NX + t
        index = jnp.where(c == 0, even, odd)
        return (mine[index].astype(F32) + arrived[index].astype(F32)).astype(BF)

    for t in range(4):
        own[t] = total(0, t)
        plus[t] = total(1, t)
        minus[t] = total(3, t)
    for t in range(2):
        two_a[t] = total(2, t)
        two_b[t] = total(2, t + 2)


def split_sum(mine, arrived):
    _, rows, columns = mine.shape
    four = jax.ShapeDtypeStruct((4, rows, columns), BF)
    two = jax.ShapeDtypeStruct((2, rows, columns), BF)
    return pl.pallas_call(
        split_kernel,
        out_shape=(four, four, four, two, two),
        in_specs=[VMEM] * 2,
        out_specs=(VMEM,) * 5,
        compiler_params=pltpu.CompilerParams(vmem_limit_bytes=24 * 2**20),
        name="split_sum",
    )(mine, arrived)


def attend_block(packed):
    head = packed.shape[-1] // 4
    scale = 1.0 / head**0.5
    query = packed[..., :head]
    keys = packed[..., head : 2 * head]
    values = packed[..., 2 * head : 3 * head]
    grad_out = packed[..., 3 * head :]
    scores = jnp.einsum("fpd,gpd->pfg", query, keys, preferred_element_type=F32) * scale
    probs = jax.nn.softmax(scores, axis=-1)
    probs_b = probs.astype(BF)
    out = jnp.einsum("pfg,gpd->fpd", probs_b, values, preferred_element_type=F32).astype(BF)
    grad_v = jnp.einsum("pfg,fpd->gpd", probs_b, grad_out, preferred_element_type=F32).astype(BF)
    grad_probs = jnp.einsum("fpd,gpd->pfg", grad_out, values, preferred_element_type=F32)
    delta = jnp.sum(grad_out.astype(F32) * out.astype(F32), axis=-1)
    grad_scores = (probs * (grad_probs - jnp.transpose(delta)[:, :, None])).astype(BF)
    grad_q = (jnp.einsum("pfg,gpd->fpd", grad_scores, keys, preferred_element_type=F32) * scale).astype(BF)
    grad_k = (jnp.einsum("pfg,fpd->gpd", grad_scores, query, preferred_element_type=F32) * scale).astype(BF)
    return jnp.concatenate([out, grad_q, grad_k, grad_v], axis=-1)


def gather(weights):
    rows, columns = weights.shape
    four = exchange(jnp.broadcast_to(weights[None], (4, rows, columns)), LIGHT)
    before = send(four, 1)
    after = send(four, -1)
    far_a = send(four[:2], 2)
    far_b = send(four[2:], -2)
    mine = jnp.concatenate([four, after, far_a, far_b, before])
    return mine, other_core(mine)


def reduce(mine, other):
    rows, columns = mine.shape[1:]
    own, plus, minus, two_a, two_b = split_sum(mine, other_core(other))
    far_a = send(two_a, 2)
    far_b = send(two_b, -2)
    from_before = send(plus, 1)
    from_after = send(minus, -1)
    total = own.astype(F32) + from_before.astype(F32) + from_after.astype(F32)
    total = total + jnp.concatenate([far_a, far_b]).astype(F32)
    pieces = total.astype(BF).reshape(4, 2, rows // 2, 4, columns // 4).transpose(0, 1, 3, 2, 4)
    pieces = pieces.reshape(4 * NZ, rows // 2, columns // 4)
    piece = jnp.sum(exchange(pieces, SPREAD).astype(F32), axis=0).astype(BF)
    copies = jnp.broadcast_to(piece[None], (NZ * NYH, *piece.shape))
    copies = lax.all_to_all(copies, ("z", "yh"), split_axis=0, concat_axis=0, tiled=True)
    copies = copies.reshape(2, 4, NYH, rows // 2, columns // 4).astype(F32)
    return jnp.sum(copies, axis=2).transpose(0, 2, 1, 3).reshape(rows, columns)


def shards(latents, cotangent, weights):
    width = latents.shape[-1]
    patches = latents.shape[2]
    columns = weights.shape[1]
    frames = NYL * NX * NC
    lat = latents.reshape(-1, width)
    cot = cotangent.reshape(-1, width)
    mine, other = gather(weights)
    packed, scale = project(mine, other, lat, cot)
    packed = packed.reshape(frames, patches // frames, columns)
    seq = ("yl", "x", "c")
    arrived = lax.all_to_all(packed, seq, split_axis=0, concat_axis=0, tiled=True)
    result = attend_block(arrived)
    back = lax.all_to_all(result, seq, split_axis=0, concat_axis=0, tiled=True)
    mine, other = weight_parts(back.reshape(-1, columns), scale, lat, cot)
    return reduce(mine, other)


def solution(mesh):
    fine = Mesh(mesh.devices.reshape(NZ, NYH, NYL, NX, NC), AXES)
    dp, seq = ("z", "yh"), ("yl", "x", "c")
    placed = (P(dp, seq, None, None), P(dp, seq, None, None), P(seq, None))
    return jax.shard_map(shards, mesh=fine, in_specs=placed, out_specs=P(seq, None), check_vma=False)
```

```python
import itertools

import jax
import jax.numpy as jnp
from jax import lax
from jax.experimental import pallas as pl
from jax.experimental.pallas import tpu as pltpu
from jax.sharding import Mesh
from jax.sharding import PartitionSpec as P

NZ, NYH, NYL, NX, NC = 8, 2, 4, 4, 2
AXES = ("z", "yh", "yl", "x", "c")
BF = jnp.bfloat16
F32 = jnp.float32
VMEM = pl.BlockSpec(memory_space=pltpu.VMEM)
ANY = pl.BlockSpec(memory_space=pl.ANY)


def device(z, yh, yl, x, c):
    return (((z * NYH + yh) * NYL + yl) * NX + x) * NC + c


def everyone():
    return itertools.product(range(NZ), range(NYH), range(NYL), range(NX), range(NC))


def groups(key, order):
    found = {}
    for at in everyone():
        found.setdefault(key(*at), []).append((order(*at), device(*at)))
    return [[d for _, d in sorted(members)] for members in found.values()]


LIGHT = groups(
    lambda z, yh, yl, x, c: (c, z, yh, yl % 2) if c else (c, z // 2, yh, x),
    lambda z, yh, yl, x, c: (yl // 2, x) if c else (yl, z % 2),
)
HEAVY = groups(
    lambda z, yh, yl, x, c: (c, z // 2, yh, yl // 2, x) if c else (c, z, yh, yl),
    lambda z, yh, yl, x, c: (yl % 2, z % 2) if c else (x,),
)
SPREAD = groups(
    lambda z, yh, yl, x, c: (c, yh, yl % 2, z % 2) if c else (c, yh, x),
    lambda z, yh, yl, x, c: (yl // 2, x, z // 2) if c else (yl, z % 2, z // 2),
)


def other_core(v):
    return lax.ppermute(v, "c", [(0, 1), (1, 0)])


def exchange(v, members):
    return lax.all_to_all(v, AXES, split_axis=0, concat_axis=0, axis_index_groups=members, tiled=True)


def half_shards():
    for yl, x, half in itertools.product(range(NYL), range(NX), range(2)):
        yield yl, x, half, x * 8 + yl * 2 + half, (yl % 2 * 2 + half) * 8 + yl // 2 * NX + x


def prepare_kernel(lat, cot, own, away):
    c = lax.axis_index("c")
    tokens, width = lat.shape
    rows = width // (NYL * NX * NC)
    block = NX * NC * rows
    part = block // 2
    source = lax.broadcasted_iota(jnp.int32, (block, block), 0)
    k = lax.broadcasted_iota(jnp.int32, (block, block), 1)
    second = (k >= part).astype(jnp.int32)
    k = k - part * second
    wanted = k + rows * (second + c - 2 * c * second)
    for b in range(1, NX):
        wanted = wanted + rows * (k >= b * rows).astype(jnp.int32)
    pick = (source == wanted).astype(F32).astype(BF)
    wide = lat[...].astype(F32)
    r = lax.rsqrt(jnp.mean(wide * wide, axis=-1, keepdims=True) + 1e-06)
    for a in range(NYL):
        at = slice(a * block, (a + 1) * block)
        to = slice(a * part, (a + 1) * part)
        normed = (lat[:, at].astype(F32) * r).astype(BF)
        for index, value in ((0, normed), (1, cot[:, at])):
            moved = jnp.dot(value, pick, preferred_element_type=F32).astype(BF)
            own[index, :, to] = moved[:, :part]
            away[index, :, to] = moved[:, part:]


def prepare(lat, cot):
    tokens, width = lat.shape
    shape = jax.ShapeDtypeStruct((2, tokens, width // 2), BF)
    return pl.pallas_call(
        prepare_kernel,
        out_shape=(shape, shape),
        in_specs=[VMEM] * 2,
        out_specs=(VMEM,) * 2,
        compiler_params=pltpu.CompilerParams(vmem_limit_bytes=24 * 2**20),
        name="prepare",
    )(lat, cot)


def project_kernel(blocks, own, arrived, mine, theirs, w, sums, sems):
    c = lax.axis_index("c")
    rows = blocks.shape[1]
    copies = []
    for yl, x, half, even, odd in half_shards():
        place = (yl * NX + x) * 2 + half
        copies.append(
            pltpu.make_async_copy(
                blocks.at[jnp.where(c == 0, even, odd)], w.at[pl.ds(place * rows, rows)], sems.at[place]
            )
        )
    for copy in copies:
        copy.start()
    for copy in copies:
        copy.wait()
    head = w.shape[1] // 4
    for index, tokens in ((0, own), (1, arrived)):
        sums[index, :, : 3 * head] = jnp.dot(tokens[0], w[:, : 3 * head], preferred_element_type=F32)
        sums[index, :, 3 * head :] = jnp.dot(tokens[1], w[:, 3 * head :], preferred_element_type=F32)
    count = own.shape[1] // 2
    for index, frame in ((0, c), (1, 1 - c)):
        for to, half in ((mine, c), (theirs, 1 - c)):
            value = sums[index, pl.ds(pl.multiple_of(half * count, 128), count), :]
            to[:, frame] = value.reshape(to.shape[0], to.shape[2], to.shape[3])


def project(blocks, own, arrived):
    _, tokens, width = own.shape
    columns = blocks.shape[-1]
    chips = NYL * NX
    shape = jax.ShapeDtypeStruct((chips, NC, tokens // (chips * NC), columns), F32)
    return pl.pallas_call(
        project_kernel,
        out_shape=(shape, shape),
        in_specs=[ANY, VMEM, VMEM],
        out_specs=(VMEM, VMEM),
        scratch_shapes=[
            pltpu.VMEM((width, columns), BF),
            pltpu.VMEM((2, tokens, columns), F32),
            pltpu.SemaphoreType.DMA((NYL * NX * 2,)),
        ],
        compiler_params=pltpu.CompilerParams(vmem_limit_bytes=24 * 2**20),
        name="project",
    )(blocks, own, arrived)


def weight_kernel(back, theirs, own, arrived, blocks, grads):
    c = lax.axis_index("c")
    chips, _, patches, columns = back.shape
    head = columns // 4
    count = chips * patches
    rows = blocks.shape[1]
    for index, frame in ((0, c), (1, 1 - c)):
        for half in range(2):
            value = jnp.where(c == half, back[:, frame].astype(F32), theirs[:, frame].astype(F32))
            grads[index, half * count : (half + 1) * count] = value.reshape(count, columns).astype(BF)
    contract = (((0,), (0,)), ((), ()))
    wide = NX * 2 * rows
    parts = []
    for yl in range(NYL):
        at = slice(yl * wide, (yl + 1) * wide)
        first, second = 0.0, 0.0
        for index, tokens in ((0, own), (1, arrived)):
            first = first + lax.dot_general(
                tokens[0, :, at], grads[index, :, head:], contract, preferred_element_type=F32
            )
            second = second + lax.dot_general(
                tokens[1, :, at], grads[index, :, :head], contract, preferred_element_type=F32
            )
        parts.append((first.astype(BF), second.astype(BF)))
    for yl, x, half, even, odd in half_shards():
        to = jnp.where(c == 0, even, odd)
        at = slice((x * 2 + half) * rows, (x * 2 + half + 1) * rows)
        blocks[to, :, : 3 * head] = parts[yl][0][at]
        blocks[to, :, 3 * head :] = parts[yl][1][at]


def weight_parts(back, theirs, own, arrived):
    _, tokens, width = own.shape
    columns = back.shape[-1]
    count = NYL * NX * 2
    return pl.pallas_call(
        weight_kernel,
        out_shape=jax.ShapeDtypeStruct((count, width // count, columns), BF),
        in_specs=[VMEM] * 4,
        out_specs=VMEM,
        scratch_shapes=[pltpu.VMEM((2, tokens, columns), BF)],
        compiler_params=pltpu.CompilerParams(vmem_limit_bytes=32 * 2**20),
        name="weight_parts",
    )(back, theirs, own, arrived)


def attend_block(packed):
    head = packed.shape[-1] // 4
    scale = 1.0 / head**0.5
    query = packed[..., :head]
    keys = packed[..., head : 2 * head]
    values = packed[..., 2 * head : 3 * head]
    grad_out = packed[..., 3 * head :]
    scores = jnp.einsum("fpd,gpd->pfg", query, keys, preferred_element_type=F32) * scale
    probs = jax.nn.softmax(scores, axis=-1)
    probs_b = probs.astype(BF)
    out = jnp.einsum("pfg,gpd->fpd", probs_b, values, preferred_element_type=F32).astype(BF)
    grad_v = jnp.einsum("pfg,fpd->gpd", probs_b, grad_out, preferred_element_type=F32).astype(BF)
    grad_probs = jnp.einsum("fpd,gpd->pfg", grad_out, values, preferred_element_type=F32)
    delta = jnp.sum(grad_out.astype(F32) * out.astype(F32), axis=-1)
    grad_scores = (probs * (grad_probs - jnp.transpose(delta)[:, :, None])).astype(BF)
    grad_q = (jnp.einsum("pfg,gpd->fpd", grad_scores, keys, preferred_element_type=F32) * scale).astype(BF)
    grad_k = (jnp.einsum("pfg,fpd->gpd", grad_scores, query, preferred_element_type=F32) * scale).astype(BF)
    return jnp.concatenate([out, grad_q, grad_k, grad_v], axis=-1)


def gather(weights):
    rows, columns = weights.shape
    half = lax.dynamic_slice_in_dim(weights, lax.rem(lax.axis_index("z"), 2) * (rows // 2), rows // 2)
    eight = exchange(jnp.broadcast_to(half[None], (8, rows // 2, columns)), LIGHT)
    blocks = exchange(jnp.broadcast_to(eight[None], (4, *eight.shape)), HEAVY)
    return blocks.reshape(32, rows // 2, columns)


def reduce(blocks):
    _, rows, columns = blocks.shape
    heavy = exchange(blocks.reshape(4, 8, rows, columns), HEAVY)
    eight = jnp.sum(heavy.astype(F32), axis=0).astype(BF)
    pieces = eight.reshape(8, rows, 4, columns // 4).transpose(0, 2, 1, 3).reshape(32, rows, columns // 4)
    piece = jnp.sum(exchange(pieces, SPREAD).astype(F32), axis=0).astype(BF)
    copies = jnp.broadcast_to(piece[None], (NZ * NYH, *piece.shape))
    copies = lax.all_to_all(copies, ("z", "yh"), split_axis=0, concat_axis=0, tiled=True)
    copies = copies.reshape(4, 2, NYH, rows, columns // 4).astype(F32)
    return jnp.sum(copies, axis=2).transpose(1, 2, 0, 3).reshape(2 * rows, columns)


def shards(latents, cotangent, weights):
    width = latents.shape[-1]
    columns = weights.shape[1]
    own, away = prepare(latents.reshape(-1, width), cotangent.reshape(-1, width))
    arrived = other_core(away)
    blocks = gather(weights)
    mine, theirs = project(blocks, own, arrived)
    packed = (mine + other_core(theirs)).astype(BF)
    plane = ("yl", "x")
    packed = lax.all_to_all(packed, plane, split_axis=0, concat_axis=0, tiled=True)
    result = attend_block(packed.reshape(-1, *packed.shape[2:]))
    back = lax.all_to_all(result.reshape(packed.shape), plane, split_axis=0, concat_axis=0, tiled=True)
    return reduce(weight_parts(back, other_core(back), own, arrived))


def solution(mesh):
    fine = Mesh(mesh.devices.reshape(NZ, NYH, NYL, NX, NC), AXES)
    dp, seq = ("z", "yh"), ("yl", "x", "c")
    placed = (P(dp, seq, None, None), P(dp, seq, None, None), P(seq, None))
    return jax.shard_map(shards, mesh=fine, in_specs=placed, out_specs=P(seq, None), check_vma=False)
```

```python
import itertools

import jax
import jax.numpy as jnp
from jax import lax
from jax.experimental import pallas as pl
from jax.experimental.pallas import tpu as pltpu
from jax.sharding import Mesh
from jax.sharding import PartitionSpec as P

NZ, NYH, NYL, NX, NC = 8, 2, 4, 4, 2
AXES = ("z", "yh", "yl", "x", "c")
BF = jnp.bfloat16
F32 = jnp.float32
VMEM = pl.BlockSpec(memory_space=pltpu.VMEM)
LIMIT = 16 * 2**20


def device(z, yh, yl, x, c):
    return (((z * NYH + yh) * NYL + yl) * NX + x) * NC + c


def everyone():
    return itertools.product(range(NZ), range(NYH), range(NYL), range(NX), range(NC))


def groups(key, order):
    found = {}
    for at in everyone():
        found.setdefault(key(*at), []).append((order(*at), device(*at)))
    return [[d for _, d in sorted(members)] for members in found.values()]


LIGHT = groups(
    lambda z, yh, yl, x, c: (c, z, yh, yl % 2) if c else (c, z // 2, yh, x),
    lambda z, yh, yl, x, c: (yl // 2, x) if c else (yl, z % 2),
)
HEAVY = groups(
    lambda z, yh, yl, x, c: (c, z // 2, yh, yl // 2, x) if c else (c, z, yh, yl),
    lambda z, yh, yl, x, c: (yl % 2, z % 2) if c else (x,),
)
SPREAD = groups(
    lambda z, yh, yl, x, c: (c, yh, yl % 2, z % 2) if c else (c, yh, x),
    lambda z, yh, yl, x, c: (yl // 2, x, z // 2) if c else (yl, z % 2, z // 2),
)


def other_core(v):
    return lax.ppermute(v, "c", [(0, 1), (1, 0)])


def exchange(v, members):
    return lax.all_to_all(v, AXES, split_axis=0, concat_axis=0, axis_index_groups=members, tiled=True)


def half_shards():
    for yl, x, half in itertools.product(range(NYL), range(NX), range(2)):
        yield yl, x, half, x * 8 + yl * 2 + half, (yl % 2 * 2 + half) * 8 + yl // 2 * NX + x


def prepare_kernel(lat, cot, own, away):
    c = lax.axis_index("c")
    tokens, width = lat.shape
    rows = width // (NYL * NX * NC)
    block = NX * NC * rows
    part = block // 2
    source = lax.broadcasted_iota(jnp.int32, (block, block), 0)
    k = lax.broadcasted_iota(jnp.int32, (block, block), 1)
    second = (k >= part).astype(jnp.int32)
    k = k - part * second
    wanted = k + rows * (second + c - 2 * c * second)
    for b in range(1, NX):
        wanted = wanted + rows * (k >= b * rows).astype(jnp.int32)
    pick = (source == wanted).astype(F32).astype(BF)
    wide = lat[...].astype(F32)
    r = lax.rsqrt(jnp.mean(wide * wide, axis=-1, keepdims=True) + 1e-06)
    for a in range(NYL):
        at = slice(a * block, (a + 1) * block)
        to = slice(a * part, (a + 1) * part)
        normed = (lat[:, at].astype(F32) * r).astype(BF)
        for index, value in ((0, normed), (1, cot[:, at])):
            moved = jnp.dot(value, pick, preferred_element_type=F32).astype(BF)
            own[index, :, to] = moved[:, :part]
            away[index, :, to] = moved[:, part:]


def prepare(lat, cot):
    tokens, width = lat.shape
    shape = jax.ShapeDtypeStruct((2, tokens, width // 2), BF)
    return pl.pallas_call(
        prepare_kernel,
        out_shape=(shape, shape),
        in_specs=[VMEM] * 2,
        out_specs=(VMEM,) * 2,
        compiler_params=pltpu.CompilerParams(vmem_limit_bytes=LIMIT),
        name="prepare",
    )(lat, cot)


def project_kernel(blocks, own, arrived, mine, theirs, w):
    c = lax.axis_index("c")
    rows = blocks.shape[1]
    for yl, x, half, even, odd in half_shards():
        place = (yl * NX + x) * 2 + half
        w[place * rows : (place + 1) * rows] = blocks[jnp.where(c == 0, even, odd)]
    head = w.shape[1] // 4
    count = own.shape[1] // 2
    shape = (mine.shape[0], mine.shape[2], 3 * head), (mine.shape[0], mine.shape[2], head)
    for tokens, frame in ((own, c), (arrived, 1 - c)):
        first = jnp.dot(tokens[0], w[:, : 3 * head], preferred_element_type=F32)
        second = jnp.dot(tokens[1], w[:, 3 * head :], preferred_element_type=F32)
        for value, at, to in (
            (first, slice(0, 3 * head), shape[0]),
            (second, slice(3 * head, 4 * head), shape[1]),
        ):
            low, high = value[:count], value[count:]
            mine[:, frame, :, at] = jnp.where(c == 0, low, high).reshape(to)
            theirs[:, frame, :, at] = jnp.where(c == 0, high, low).reshape(to)


def project(blocks, own, arrived):
    _, tokens, width = own.shape
    columns = blocks.shape[-1]
    chips = NYL * NX
    shape = jax.ShapeDtypeStruct((chips, NC, tokens // (chips * NC), columns), F32)
    return pl.pallas_call(
        project_kernel,
        out_shape=(shape, shape),
        in_specs=[VMEM] * 3,
        out_specs=(VMEM, VMEM),
        scratch_shapes=[pltpu.VMEM((width, columns), BF)],
        compiler_params=pltpu.CompilerParams(vmem_limit_bytes=LIMIT),
        name="project",
    )(blocks, own, arrived)


def weight_kernel(back, theirs, own, arrived, blocks, grads):
    c = lax.axis_index("c")
    chips, _, patches, columns = back.shape
    head = columns // 4
    count = chips * patches
    rows = blocks.shape[1]
    for index, frame in ((0, c), (1, 1 - c)):
        for half in range(2):
            value = jnp.where(c == half, back[:, frame].astype(F32), theirs[:, frame].astype(F32))
            grads[index, half * count : (half + 1) * count] = value.reshape(count, columns).astype(BF)
    contract = (((0,), (0,)), ((), ()))
    wide = NX * 2 * rows
    parts = []
    for yl in range(NYL):
        at = slice(yl * wide, (yl + 1) * wide)
        first, second = 0.0, 0.0
        for index, tokens in ((0, own), (1, arrived)):
            first = first + lax.dot_general(
                tokens[0, :, at], grads[index, :, head:], contract, preferred_element_type=F32
            )
            second = second + lax.dot_general(
                tokens[1, :, at], grads[index, :, :head], contract, preferred_element_type=F32
            )
        parts.append((first.astype(BF), second.astype(BF)))
    for yl, x, half, even, odd in half_shards():
        to = jnp.where(c == 0, even, odd)
        at = slice((x * 2 + half) * rows, (x * 2 + half + 1) * rows)
        blocks[to, :, : 3 * head] = parts[yl][0][at]
        blocks[to, :, 3 * head :] = parts[yl][1][at]


def weight_parts(back, theirs, own, arrived):
    _, tokens, width = own.shape
    columns = back.shape[-1]
    count = NYL * NX * 2
    return pl.pallas_call(
        weight_kernel,
        out_shape=jax.ShapeDtypeStruct((count, width // count, columns), BF),
        in_specs=[VMEM] * 4,
        out_specs=VMEM,
        scratch_shapes=[pltpu.VMEM((2, tokens, columns), BF)],
        compiler_params=pltpu.CompilerParams(vmem_limit_bytes=LIMIT),
        name="weight_parts",
    )(back, theirs, own, arrived)


def attend_kernel(packed, result):
    tokens, columns = packed.shape
    head = columns // 4
    scale = 1.0 / head**0.5
    patches = tokens // (NYL * NX * NC)
    query, keys, values, grad_out = (packed[:, i * head : (i + 1) * head] for i in range(4))
    row = lax.broadcasted_iota(jnp.int32, (tokens, tokens), 0)
    column = lax.broadcasted_iota(jnp.int32, (tokens, tokens), 1)
    same = lax.rem(row, patches) == lax.rem(column, patches)
    across, down = (((1,), (1,)), ((), ())), (((0,), (0,)), ((), ()))
    scores = lax.dot_general(query, keys, across, preferred_element_type=F32) * scale
    scores = jnp.where(same, scores, -jnp.inf)
    weights = jnp.exp(scores - jnp.max(scores, axis=-1, keepdims=True))
    probs = weights / jnp.sum(weights, axis=-1, keepdims=True)
    probs_b = probs.astype(BF)
    out = jnp.dot(probs_b, values, preferred_element_type=F32).astype(BF)
    result[:, :head] = out
    grad_v = lax.dot_general(probs_b, grad_out, down, preferred_element_type=F32)
    result[:, 3 * head :] = grad_v.astype(BF)
    grad_probs = lax.dot_general(grad_out, values, across, preferred_element_type=F32)
    delta = jnp.sum(grad_out.astype(F32) * out.astype(F32), axis=-1, keepdims=True)
    grad_scores = jnp.where(same, probs * (grad_probs - delta), 0.0).astype(BF)
    grad_q = jnp.dot(grad_scores, keys, preferred_element_type=F32) * scale
    result[:, head : 2 * head] = grad_q.astype(BF)
    grad_k = lax.dot_general(grad_scores, query, down, preferred_element_type=F32) * scale
    result[:, 2 * head : 3 * head] = grad_k.astype(BF)


def attend(packed):
    return pl.pallas_call(
        attend_kernel,
        out_shape=jax.ShapeDtypeStruct(packed.shape, BF),
        in_specs=[VMEM],
        out_specs=VMEM,
        compiler_params=pltpu.CompilerParams(vmem_limit_bytes=LIMIT),
        name="attend",
    )(packed)


def gather(weights, own):
    rows, columns = weights.shape
    half = lax.dynamic_slice_in_dim(weights, lax.rem(lax.axis_index("z"), 2) * (rows // 2), rows // 2)
    eight = exchange(jnp.broadcast_to(half[None], (8, rows // 2, columns)), LIGHT)
    eight, own = lax.optimization_barrier((eight, own))
    blocks = exchange(jnp.broadcast_to(eight[None], (4, *eight.shape)), HEAVY)
    return blocks.reshape(32, rows // 2, columns), own


def reduce(blocks):
    _, rows, columns = blocks.shape
    heavy = exchange(blocks.reshape(4, 8, rows, columns), HEAVY)
    eight = jnp.sum(heavy.astype(F32), axis=0).astype(BF)
    pieces = eight.reshape(8, rows, 4, columns // 4).transpose(0, 2, 1, 3).reshape(32, rows, columns // 4)
    piece = jnp.sum(exchange(pieces, SPREAD).astype(F32), axis=0).astype(BF)
    copies = jnp.broadcast_to(piece[None], (NZ * NYH, *piece.shape))
    copies = lax.all_to_all(copies, ("z", "yh"), split_axis=0, concat_axis=0, tiled=True)
    copies = copies.reshape(4, 2, NYH, rows, columns // 4).astype(F32)
    return jnp.sum(copies, axis=2).transpose(1, 2, 0, 3).reshape(2 * rows, columns)


def shards(latents, cotangent, weights):
    width = latents.shape[-1]
    columns = weights.shape[1]
    own, away = prepare(latents.reshape(-1, width), cotangent.reshape(-1, width))
    arrived = other_core(away)
    blocks, own = gather(weights, own)
    mine, theirs = project(blocks, own, arrived)
    packed = (mine + other_core(theirs)).astype(BF)
    plane = ("yl", "x")
    packed = lax.all_to_all(packed, plane, split_axis=0, concat_axis=0, tiled=True)
    result = attend(packed.reshape(-1, columns))
    back = lax.all_to_all(result.reshape(packed.shape), plane, split_axis=0, concat_axis=0, tiled=True)
    return reduce(weight_parts(back, other_core(back), own, arrived))


def solution(mesh):
    fine = Mesh(mesh.devices.reshape(NZ, NYH, NYL, NX, NC), AXES)
    dp, seq = ("z", "yh"), ("yl", "x", "c")
    placed = (P(dp, seq, None, None), P(dp, seq, None, None), P(seq, None))
    return jax.shard_map(shards, mesh=fine, in_specs=placed, out_specs=P(seq, None), check_vma=False)
```

```python
import functools
import itertools

import jax
import jax.numpy as jnp
from jax import lax
from jax.experimental import pallas as pl
from jax.experimental.pallas import tpu as pltpu
from jax.sharding import Mesh
from jax.sharding import PartitionSpec as P

NZ, NYH, NYL, NX, NC = 8, 2, 4, 4, 2
AXES = ("z", "yh", "yl", "x", "c")
BF = jnp.bfloat16
F32 = jnp.float32
VMEM = pl.BlockSpec(memory_space=pltpu.VMEM)
HBM = pl.BlockSpec(memory_space=pltpu.HBM)
LIMIT = 16 * 2**20


def device(z, yh, yl, x, c):
    return (((z * NYH + yh) * NYL + yl) * NX + x) * NC + c


def everyone():
    return itertools.product(range(NZ), range(NYH), range(NYL), range(NX), range(NC))


def groups(key, order):
    found = {}
    for at in everyone():
        found.setdefault(key(*at), []).append((order(*at), device(*at)))
    return [[d for _, d in sorted(members)] for members in found.values()]


def cube_groups(key, order):
    def named(names):
        def value(z, yh, yl, x, c):
            zs, ys, xs = (z + c) % NZ, (yh * NYL + yl + c) % (NYH * NYL), (x + c) % NX
            place = {"z1": zs // 2, "z0": zs % 2, "y2": ys // 4, "y1": ys // 2 % 2, "y0": ys % 2}
            place |= {"x1": xs // 2, "x0": xs % 2, "yl": yl, "x": x, "c": c}
            return tuple(place[name] for name in names)

        return value

    return groups(named(key), named(order))


LIGHT = cube_groups(("c", "z1", "z0", "y2", "y0", "x0"), ("y1", "x1"))
HEAVY = cube_groups(("c", "z1", "y2", "y1", "x1"), ("y0", "x0", "z0"))
SPREAD = cube_groups(("c", "y2", "y0", "x0", "z0"), ("y1", "x1", "z1"))
COPIES = cube_groups(("c", "yl", "x"), ("z1", "z0", "y2"))
PLANE = groups(
    lambda z, yh, yl, x, c: (z, yh, c),
    lambda z, yh, yl, x, c: ((yl + 2 * c) % NYL, (x + 2 * c) % NX),
)


def other_core(v):
    return lax.ppermute(v, "c", [(0, 1), (1, 0)])


def exchange(v, members):
    return lax.all_to_all(v, AXES, split_axis=0, concat_axis=0, axis_index_groups=members, tiled=True)


def half_shards():
    for yl, x, half in itertools.product(range(NYL), range(NX), range(2)):
        places = []
        for c in range(NC):
            ys, xs = (yl + c) % NYL, (x + c) % NX
            places.append((((ys % 2 * 2 + xs % 2) * 2 + half) * 2 + ys // 2) * 2 + xs // 2)
        yield yl, x, half, *places


def prepare_kernel(norm, value, own, away):
    c = lax.axis_index("c")
    width = value.shape[1]
    rows = width // (NYL * NX * NC)
    block = NX * NC * rows
    part = block // 2
    source = lax.broadcasted_iota(jnp.int32, (block, block), 0)
    k = lax.broadcasted_iota(jnp.int32, (block, block), 1)
    second = (k >= part).astype(jnp.int32)
    k = k - part * second
    wanted = k + rows * (second + c - 2 * c * second)
    for b in range(1, NX):
        wanted = wanted + rows * (k >= b * rows).astype(jnp.int32)
    pick = (source == wanted).astype(F32).astype(BF)
    if norm:
        wide = value[...].astype(F32)
        r = lax.rsqrt(jnp.mean(wide * wide, axis=-1, keepdims=True) + 1e-06)
    for a in range(NYL):
        tokens = value[:, a * block : (a + 1) * block]
        if norm:
            tokens = (tokens.astype(F32) * r).astype(BF)
        moved = jnp.dot(tokens, pick, preferred_element_type=F32).astype(BF)
        own[:, a * part : (a + 1) * part] = moved[:, :part]
        away[:, a * part : (a + 1) * part] = moved[:, part:]


def prepare(value, norm):
    tokens, width = value.shape
    shape = jax.ShapeDtypeStruct((tokens, width // 2), BF)
    return pl.pallas_call(
        functools.partial(prepare_kernel, norm),
        out_shape=(shape, shape),
        in_specs=[VMEM],
        out_specs=(VMEM, VMEM),
        compiler_params=pltpu.CompilerParams(vmem_limit_bytes=LIMIT),
        name="prepare",
    )(value)


def multiply(lat, cot, w, mine, theirs):
    c = lax.axis_index("c")
    head = w.shape[1] // 4
    count = lat.shape[0] // 2
    for tokens, at in ((lat, slice(0, 3 * head)), (cot, slice(3 * head, 4 * head))):
        value = jnp.dot(tokens[...], w[:, at], preferred_element_type=F32)
        to = (mine.shape[0], mine.shape[1], at.stop - at.start)
        low, high = value[:count], value[count:]
        mine[:, :, at] = jnp.where(c == 0, low, high).reshape(to)
        theirs[:, :, at] = jnp.where(c == 0, high, low).reshape(to).astype(BF)


def project_own_kernel(blocks, lat, cot, w, mine, theirs):
    c = lax.axis_index("c")
    rows = blocks.shape[1]
    for yl, x, half, even, odd in half_shards():
        place = (yl * NX + x) * 2 + half
        w[place * rows : (place + 1) * rows] = blocks[jnp.where(c == 0, even, odd)]
    multiply(lat, cot, w, mine, theirs)


def project_both_kernel(w, lat, cot, own_mine, own_theirs, mine, theirs, new_mine, new_theirs):
    c = lax.axis_index("c")
    multiply(lat, cot, w, new_mine, new_theirs)
    for own, new, to in ((own_mine, new_mine, mine), (own_theirs, new_theirs, theirs)):
        to[:, c] = own[...]
        to[:, 1 - c] = new[...]


def project(blocks, own_l, own_c, arr_l, arr_c):
    tokens, width = own_l.shape
    columns = blocks.shape[-1]
    chips = NYL * NX
    rows = tokens // (chips * NC)
    half, whole = (chips, rows, columns), (chips, NC, rows, columns)
    params = pltpu.CompilerParams(vmem_limit_bytes=LIMIT)
    w, mine, theirs = pl.pallas_call(
        project_own_kernel,
        out_shape=(
            jax.ShapeDtypeStruct((width, columns), BF),
            jax.ShapeDtypeStruct(half, F32),
            jax.ShapeDtypeStruct(half, BF),
        ),
        in_specs=[VMEM] * 3,
        out_specs=(VMEM,) * 3,
        compiler_params=params,
        name="project_own",
    )(blocks, own_l, own_c)
    return pl.pallas_call(
        project_both_kernel,
        out_shape=(jax.ShapeDtypeStruct(whole, F32), jax.ShapeDtypeStruct(whole, BF)),
        in_specs=[VMEM] * 5,
        out_specs=(VMEM,) * 2,
        scratch_shapes=[pltpu.VMEM(half, F32), pltpu.VMEM(half, BF)],
        compiler_params=params,
        name="project_both",
    )(w, arr_l, arr_c, mine, theirs)


def weight_kernel(columns, back, own, arrived, *rest):
    blocks, grads = rest[-2:]
    c = lax.axis_index("c")
    _, chips, _, patches, _ = back.shape
    count = chips * patches
    rows = blocks.shape[1]
    source, to = columns
    for index, frame in ((0, c), (1, 1 - c)):
        for half in range(2):
            value = back[half, :, frame, :, source].astype(F32)
            grads[index, half * count : (half + 1) * count] = value.reshape(count, -1).astype(BF)
    wide = NX * 2 * rows
    for yl in range(NYL):
        part = slice(yl * wide, (yl + 1) * wide)
        value = 0.0
        for index, tokens in ((0, own), (1, arrived)):
            value = value + lax.dot_general(
                tokens[:, part], grads[index], (((0,), (0,)), ((), ())), preferred_element_type=F32
            )
        value = value.astype(BF)
        for y, x, half, even, odd in half_shards():
            if y == yl:
                piece = value[(x * 2 + half) * rows : (x * 2 + half + 1) * rows]
                blocks[jnp.where(c == 0, even, odd), :, to] = piece


def weight_parts(back, own_l, own_c, arr_l, arr_c):
    tokens, width = own_l.shape
    columns = back.shape[-1]
    head = columns // 4
    count = NYL * NX * 2

    def call(source, to, own, arrived, *blocks):
        return pl.pallas_call(
            functools.partial(weight_kernel, (source, to)),
            out_shape=jax.ShapeDtypeStruct((count, width // count, columns), BF),
            in_specs=[VMEM] * (3 + len(blocks)),
            out_specs=VMEM,
            scratch_shapes=[pltpu.VMEM((2, tokens, source.stop - source.start), BF)],
            input_output_aliases={3: 0} if blocks else {},
            compiler_params=pltpu.CompilerParams(vmem_limit_bytes=LIMIT),
            name="weight_parts",
        )(back, own, arrived, *blocks)

    blocks = call(slice(head, 4 * head), slice(0, 3 * head), own_l, arr_l)
    return call(slice(0, head), slice(3 * head, 4 * head), own_c, arr_c, blocks)


def attend_kernel(packed, result):
    tokens, columns = packed.shape
    head = columns // 4
    scale = 1.0 / head**0.5
    patches = tokens // (NYL * NX * NC)
    query, keys, values, grad_out = (packed[:, i * head : (i + 1) * head] for i in range(4))
    row = lax.broadcasted_iota(jnp.int32, (tokens, tokens), 0)
    column = lax.broadcasted_iota(jnp.int32, (tokens, tokens), 1)
    same = lax.rem(row, patches) == lax.rem(column, patches)
    across, down = (((1,), (1,)), ((), ())), (((0,), (0,)), ((), ()))
    scores = lax.dot_general(query, keys, across, preferred_element_type=F32) * scale
    scores = jnp.where(same, scores, -jnp.inf)
    weights = jnp.exp(scores - jnp.max(scores, axis=-1, keepdims=True))
    probs = weights / jnp.sum(weights, axis=-1, keepdims=True)
    probs_b = probs.astype(BF)
    out = jnp.dot(probs_b, values, preferred_element_type=F32).astype(BF)
    result[:, :head] = out
    grad_v = lax.dot_general(probs_b, grad_out, down, preferred_element_type=F32)
    result[:, 3 * head :] = grad_v.astype(BF)
    grad_probs = lax.dot_general(grad_out, values, across, preferred_element_type=F32)
    delta = jnp.sum(grad_out.astype(F32) * out.astype(F32), axis=-1, keepdims=True)
    grad_scores = jnp.where(same, probs * (grad_probs - delta), 0.0).astype(BF)
    grad_q = jnp.dot(grad_scores, keys, preferred_element_type=F32) * scale
    result[:, head : 2 * head] = grad_q.astype(BF)
    grad_k = lax.dot_general(grad_scores, query, down, preferred_element_type=F32) * scale
    result[:, 2 * head : 3 * head] = grad_k.astype(BF)


def attend(packed):
    return pl.pallas_call(
        attend_kernel,
        out_shape=jax.ShapeDtypeStruct(packed.shape, BF),
        in_specs=[VMEM],
        out_specs=VMEM,
        compiler_params=pltpu.CompilerParams(vmem_limit_bytes=LIMIT),
        name="attend",
    )(packed)


def repeat_kernel(value, copies, sems):
    started = [pltpu.make_async_copy(value, copies.at[i], sems.at[i]) for i in range(copies.shape[0])]
    for copy in started:
        copy.start()
    for copy in started:
        copy.wait()


def repeat(value, count):
    return pl.pallas_call(
        repeat_kernel,
        out_shape=jax.ShapeDtypeStruct((count, *value.shape), value.dtype),
        in_specs=[VMEM],
        out_specs=HBM,
        scratch_shapes=[pltpu.SemaphoreType.DMA((count,))],
        compiler_params=pltpu.CompilerParams(vmem_limit_bytes=LIMIT),
        name="repeat",
    )(value)


def finish_kernel(copies, total):
    _, _, rows, columns = copies.shape
    for z1, z0 in itertools.product(range(NZ // 2), range(2)):
        index = z1 * 2 + z0
        value = copies[index, 0].astype(F32) + copies[index, 1].astype(F32)
        total[z0 * rows : (z0 + 1) * rows, z1 * columns : (z1 + 1) * columns] = value


def finish(copies):
    _, _, rows, columns = copies.shape
    return pl.pallas_call(
        finish_kernel,
        out_shape=jax.ShapeDtypeStruct((2 * rows, NZ // 2 * columns), F32),
        in_specs=[VMEM],
        out_specs=VMEM,
        compiler_params=pltpu.CompilerParams(vmem_limit_bytes=LIMIT),
        name="finish",
    )(copies)


def gather(weights, own):
    rows, columns = weights.shape
    z0 = lax.rem(lax.axis_index("z") + lax.axis_index("c"), 2)
    half = lax.dynamic_slice_in_dim(weights, z0 * (rows // 2), rows // 2)
    four = exchange(jnp.broadcast_to(half[None], (4, rows // 2, columns)), LIGHT)
    four, own = lax.optimization_barrier((four, own))
    blocks = exchange(repeat(four, 8), HEAVY)
    return blocks.reshape(32, rows // 2, columns), own


def reduce(blocks):
    _, rows, columns = blocks.shape
    heavy = exchange(blocks.reshape(8, 4, rows, columns), HEAVY)
    four = jnp.sum(heavy.astype(F32), axis=0).astype(BF)
    pieces = four.reshape(4, rows, 4, columns // 4).transpose(0, 2, 1, 3).reshape(16, rows, columns // 4)
    piece = jnp.sum(exchange(pieces, SPREAD).astype(F32), axis=0).astype(BF)
    copies = exchange(jnp.broadcast_to(piece[None], (NZ * NYH, *piece.shape)), COPIES)
    return finish(copies.reshape(NZ, NYH, *piece.shape))


def shards(latents, cotangent, weights):
    width = latents.shape[-1]
    columns = weights.shape[1]
    own_l, away_l = prepare(latents.reshape(-1, width), True)
    own_c, away_c = prepare(cotangent.reshape(-1, width), False)
    blocks, own_l = gather(weights, own_l)
    tokens = own_l, own_c, other_core(away_l), other_core(away_c)
    mine, theirs = project(blocks, *tokens)
    both = lax.all_gather(theirs, "c")
    part = lax.dynamic_index_in_dim(both, 1 - lax.axis_index("c"), keepdims=False)
    packed = exchange((mine + part.astype(F32)).astype(BF), PLANE)
    result = attend(packed.reshape(-1, columns))
    back = lax.all_gather(exchange(result.reshape(packed.shape), PLANE), "c")
    return reduce(weight_parts(back, *tokens))


def solution(mesh):
    fine = Mesh(mesh.devices.reshape(NZ, NYH, NYL, NX, NC), AXES)
    dp, seq = ("z", "yh"), ("yl", "x", "c")
    placed = (P(dp, seq, None, None), P(dp, seq, None, None), P(seq, None))
    return jax.shard_map(shards, mesh=fine, in_specs=placed, out_specs=P(seq, None), check_vma=False)
```

```python
import functools
import itertools

import jax
import jax.numpy as jnp
from jax import lax
from jax.experimental import pallas as pl
from jax.experimental.pallas import tpu as pltpu
from jax.sharding import Mesh
from jax.sharding import PartitionSpec as P

NZ, NYH, NYL, NX, NC = 8, 2, 4, 4, 2
AXES = ("z", "yh", "yl", "x", "c")
BF = jnp.bfloat16
F32 = jnp.float32
VMEM = pl.BlockSpec(memory_space=pltpu.VMEM)
HBM = pl.BlockSpec(memory_space=pltpu.HBM)
LIMIT = 16 * 2**20


def device(z, yh, yl, x, c):
    return (((z * NYH + yh) * NYL + yl) * NX + x) * NC + c


def everyone():
    return itertools.product(range(NZ), range(NYH), range(NYL), range(NX), range(NC))


def groups(key, order):
    found = {}
    for at in everyone():
        found.setdefault(key(*at), []).append((order(*at), device(*at)))
    return [[d for _, d in sorted(members)] for members in found.values()]


def cube_groups(key, order):
    def named(names):
        def value(z, yh, yl, x, c):
            zs, ys, xs = (z + c) % NZ, (yh * NYL + yl + c) % (NYH * NYL), (x + c) % NX
            place = {"z1": zs // 2, "z0": zs % 2, "y2": ys // 4, "y1": ys // 2 % 2, "y0": ys % 2}
            place |= {"x1": xs // 2, "x0": xs % 2, "yl": yl, "x": x, "c": c}
            return tuple(place[name] for name in names)

        return value

    return groups(named(key), named(order))


LIGHT = cube_groups(("c", "z1", "z0", "y2", "y0", "x0"), ("y1", "x1"))
HEAVY = cube_groups(("c", "z1", "y2", "y1", "x1"), ("y0", "x0", "z0"))
SPREAD = cube_groups(("c", "y2", "y0", "x0", "z0"), ("y1", "x1", "z1"))
COPIES = cube_groups(("c", "yl", "x"), ("z1", "z0", "y2"))
PLANE = groups(
    lambda z, yh, yl, x, c: (z, yh, c),
    lambda z, yh, yl, x, c: ((yl + 1 + 2 * c) % NYL, (x + 2 * c) % NX),
)


def other_core(v):
    return lax.ppermute(v, "c", [(0, 1), (1, 0)])


def exchange(v, members):
    return lax.all_to_all(v, AXES, split_axis=0, concat_axis=0, axis_index_groups=members, tiled=True)


def half_shards():
    for yl, x, half in itertools.product(range(NYL), range(NX), range(2)):
        places = []
        for c in range(NC):
            ys, xs = (yl + c) % NYL, (x + c) % NX
            places.append((((ys % 2 * 2 + xs % 2) * 2 + half) * 2 + ys // 2) * 2 + xs // 2)
        yield yl, x, half, *places


def prepare_kernel(norm, value, own, away):
    c = lax.axis_index("c")
    width = value.shape[1]
    rows = width // (NYL * NX * NC)
    block = NX * NC * rows
    part = block // 2
    source = lax.broadcasted_iota(jnp.int32, (block, block), 0)
    k = lax.broadcasted_iota(jnp.int32, (block, block), 1)
    second = (k >= part).astype(jnp.int32)
    k = k - part * second
    wanted = k + rows * (second + c - 2 * c * second)
    for b in range(1, NX):
        wanted = wanted + rows * (k >= b * rows).astype(jnp.int32)
    pick = (source == wanted).astype(F32).astype(BF)
    if norm:
        wide = value[...].astype(F32)
        r = lax.rsqrt(jnp.mean(wide * wide, axis=-1, keepdims=True) + 1e-06)
    for a in range(NYL):
        tokens = value[:, a * block : (a + 1) * block]
        if norm:
            tokens = (tokens.astype(F32) * r).astype(BF)
        moved = jnp.dot(tokens, pick, preferred_element_type=F32).astype(BF)
        own[:, a * part : (a + 1) * part] = moved[:, :part]
        away[:, a * part : (a + 1) * part] = moved[:, part:]


def prepare(value, norm):
    tokens, width = value.shape
    shape = jax.ShapeDtypeStruct((tokens, width // 2), BF)
    return pl.pallas_call(
        functools.partial(prepare_kernel, norm),
        out_shape=(shape, shape),
        in_specs=[VMEM],
        out_specs=(VMEM, VMEM),
        compiler_params=pltpu.CompilerParams(vmem_limit_bytes=LIMIT),
        name="prepare",
    )(value)


def multiply(lat, cot, w, mine, theirs):
    c = lax.axis_index("c")
    head = w.shape[1] // 4
    count = lat.shape[0] // 2
    for tokens, at in ((lat, slice(0, 3 * head)), (cot, slice(3 * head, 4 * head))):
        value = jnp.dot(tokens[...], w[:, at], preferred_element_type=F32)
        to = (mine.shape[0], mine.shape[1], at.stop - at.start)
        low, high = value[:count], value[count:]
        mine[:, :, at] = jnp.where(c == 0, low, high).reshape(to)
        theirs[:, :, at] = jnp.where(c == 0, high, low).reshape(to).astype(BF)


def project_own_kernel(blocks, lat, cot, w, mine, theirs):
    c = lax.axis_index("c")
    rows = blocks.shape[1]
    for yl, x, half, even, odd in half_shards():
        place = (yl * NX + x) * 2 + half
        w[place * rows : (place + 1) * rows] = blocks[jnp.where(c == 0, even, odd)]
    multiply(lat, cot, w, mine, theirs)


def project_both_kernel(w, lat, cot, own_mine, own_theirs, mine, theirs, new_mine, new_theirs):
    c = lax.axis_index("c")
    multiply(lat, cot, w, new_mine, new_theirs)
    for own, new, to in ((own_mine, new_mine, mine), (own_theirs, new_theirs, theirs)):
        to[:, c] = own[...]
        to[:, 1 - c] = new[...]


def project(blocks, own_l, own_c, arr_l, arr_c):
    tokens, width = own_l.shape
    columns = blocks.shape[-1]
    chips = NYL * NX
    rows = tokens // (chips * NC)
    half, whole = (chips, rows, columns), (chips, NC, rows, columns)
    params = pltpu.CompilerParams(vmem_limit_bytes=LIMIT)
    w, mine, theirs = pl.pallas_call(
        project_own_kernel,
        out_shape=(
            jax.ShapeDtypeStruct((width, columns), BF),
            jax.ShapeDtypeStruct(half, F32),
            jax.ShapeDtypeStruct(half, BF),
        ),
        in_specs=[VMEM] * 3,
        out_specs=(VMEM,) * 3,
        compiler_params=params,
        name="project_own",
    )(blocks, own_l, own_c)
    return pl.pallas_call(
        project_both_kernel,
        out_shape=(jax.ShapeDtypeStruct(whole, F32), jax.ShapeDtypeStruct(whole, BF)),
        in_specs=[VMEM] * 5,
        out_specs=(VMEM,) * 2,
        scratch_shapes=[pltpu.VMEM(half, F32), pltpu.VMEM(half, BF)],
        compiler_params=params,
        name="project_both",
    )(w, arr_l, arr_c, mine, theirs)


def weight_kernel(columns, back, own, arrived, *rest):
    blocks, grads = rest[-2:]
    c = lax.axis_index("c")
    _, chips, _, patches, _ = back.shape
    count = chips * patches
    rows = blocks.shape[1]
    source, to = columns
    for index, frame in ((0, c), (1, 1 - c)):
        for half in range(2):
            value = back[half, :, frame, :, source].astype(F32)
            grads[index, half * count : (half + 1) * count] = value.reshape(count, -1).astype(BF)
    wide = NX * 2 * rows
    for yl in range(NYL):
        part = slice(yl * wide, (yl + 1) * wide)
        value = 0.0
        for index, tokens in ((0, own), (1, arrived)):
            value = value + lax.dot_general(
                tokens[:, part], grads[index], (((0,), (0,)), ((), ())), preferred_element_type=F32
            )
        value = value.astype(BF)
        for y, x, half, even, odd in half_shards():
            if y == yl:
                piece = value[(x * 2 + half) * rows : (x * 2 + half + 1) * rows]
                blocks[jnp.where(c == 0, even, odd), :, to] = piece


def weight_parts(back, own_l, own_c, arr_l, arr_c):
    tokens, width = own_l.shape
    columns = back.shape[-1]
    head = columns // 4
    count = NYL * NX * 2

    def call(source, to, own, arrived, *blocks):
        return pl.pallas_call(
            functools.partial(weight_kernel, (source, to)),
            out_shape=jax.ShapeDtypeStruct((count, width // count, columns), BF),
            in_specs=[VMEM] * (3 + len(blocks)),
            out_specs=VMEM,
            scratch_shapes=[pltpu.VMEM((2, tokens, source.stop - source.start), BF)],
            input_output_aliases={3: 0} if blocks else {},
            compiler_params=pltpu.CompilerParams(vmem_limit_bytes=LIMIT),
            name="weight_parts",
        )(back, own, arrived, *blocks)

    blocks = call(slice(head, 4 * head), slice(0, 3 * head), own_l, arr_l)
    return call(slice(0, head), slice(3 * head, 4 * head), own_c, arr_c, blocks)


def attend_kernel(packed, result):
    tokens, columns = packed.shape
    head = columns // 4
    scale = 1.0 / head**0.5
    patches = tokens // (NYL * NX * NC)
    query, keys, values, grad_out = (packed[:, i * head : (i + 1) * head] for i in range(4))
    row = lax.broadcasted_iota(jnp.int32, (tokens, tokens), 0)
    column = lax.broadcasted_iota(jnp.int32, (tokens, tokens), 1)
    same = lax.rem(row, patches) == lax.rem(column, patches)
    across, down = (((1,), (1,)), ((), ())), (((0,), (0,)), ((), ()))
    scores = lax.dot_general(query, keys, across, preferred_element_type=F32) * scale
    scores = jnp.where(same, scores, -jnp.inf)
    weights = jnp.exp(scores - jnp.max(scores, axis=-1, keepdims=True))
    probs = weights / jnp.sum(weights, axis=-1, keepdims=True)
    probs_b = probs.astype(BF)
    out = jnp.dot(probs_b, values, preferred_element_type=F32).astype(BF)
    result[:, :head] = out
    grad_v = lax.dot_general(probs_b, grad_out, down, preferred_element_type=F32)
    result[:, 3 * head :] = grad_v.astype(BF)
    grad_probs = lax.dot_general(grad_out, values, across, preferred_element_type=F32)
    delta = jnp.sum(grad_out.astype(F32) * out.astype(F32), axis=-1, keepdims=True)
    grad_scores = jnp.where(same, probs * (grad_probs - delta), 0.0).astype(BF)
    grad_q = jnp.dot(grad_scores, keys, preferred_element_type=F32) * scale
    result[:, head : 2 * head] = grad_q.astype(BF)
    grad_k = lax.dot_general(grad_scores, query, down, preferred_element_type=F32) * scale
    result[:, 2 * head : 3 * head] = grad_k.astype(BF)


def attend(packed):
    return pl.pallas_call(
        attend_kernel,
        out_shape=jax.ShapeDtypeStruct(packed.shape, BF),
        in_specs=[VMEM],
        out_specs=VMEM,
        compiler_params=pltpu.CompilerParams(vmem_limit_bytes=LIMIT),
        name="attend",
    )(packed)


def repeat_kernel(value, copies, sems):
    started = [pltpu.make_async_copy(value, copies.at[i], sems.at[i]) for i in range(copies.shape[0])]
    for copy in started:
        copy.start()
    for copy in started:
        copy.wait()


def repeat(value, count):
    return pl.pallas_call(
        repeat_kernel,
        out_shape=jax.ShapeDtypeStruct((count, *value.shape), value.dtype),
        in_specs=[VMEM],
        out_specs=HBM,
        scratch_shapes=[pltpu.SemaphoreType.DMA((count,))],
        compiler_params=pltpu.CompilerParams(vmem_limit_bytes=LIMIT),
        name="repeat",
    )(value)


def finish_kernel(copies, total):
    _, _, rows, columns = copies.shape
    for z1, z0 in itertools.product(range(NZ // 2), range(2)):
        index = z1 * 2 + z0
        value = copies[index, 0].astype(F32) + copies[index, 1].astype(F32)
        total[z0 * rows : (z0 + 1) * rows, z1 * columns : (z1 + 1) * columns] = value


def finish(copies):
    _, _, rows, columns = copies.shape
    return pl.pallas_call(
        finish_kernel,
        out_shape=jax.ShapeDtypeStruct((2 * rows, NZ // 2 * columns), F32),
        in_specs=[VMEM],
        out_specs=VMEM,
        compiler_params=pltpu.CompilerParams(vmem_limit_bytes=LIMIT),
        name="finish",
    )(copies)


def gather(weights, own):
    rows, columns = weights.shape
    z0 = lax.rem(lax.axis_index("z") + lax.axis_index("c"), 2)
    half = lax.dynamic_slice_in_dim(weights, z0 * (rows // 2), rows // 2)
    four = exchange(jnp.broadcast_to(half[None], (4, rows // 2, columns)), LIGHT)
    four, own = lax.optimization_barrier((four, own))
    blocks = exchange(repeat(four, 8), HEAVY)
    return blocks.reshape(32, rows // 2, columns), own


def reduce(blocks):
    _, rows, columns = blocks.shape
    heavy = exchange(blocks.reshape(8, 4, rows, columns), HEAVY)
    four = jnp.sum(heavy.astype(F32), axis=0).astype(BF)
    pieces = four.reshape(4, rows, 4, columns // 4).transpose(0, 2, 1, 3).reshape(16, rows, columns // 4)
    piece = jnp.sum(exchange(pieces, SPREAD).astype(F32), axis=0).astype(BF)
    copies = exchange(jnp.broadcast_to(piece[None], (NZ * NYH, *piece.shape)), COPIES)
    return finish(copies.reshape(NZ, NYH, *piece.shape))


def shards(latents, cotangent, weights):
    width = latents.shape[-1]
    columns = weights.shape[1]
    own_l, away_l = prepare(latents.reshape(-1, width), True)
    own_c, away_c = prepare(cotangent.reshape(-1, width), False)
    blocks, own_l = gather(weights, own_l)
    tokens = own_l, own_c, other_core(away_l), other_core(away_c)
    mine, theirs = project(blocks, *tokens)
    both = lax.all_gather(theirs, "c")
    part = lax.dynamic_index_in_dim(both, 1 - lax.axis_index("c"), keepdims=False)
    packed = exchange((mine + part.astype(F32)).astype(BF), PLANE)
    result = attend(packed.reshape(-1, columns))
    back = lax.all_gather(exchange(result.reshape(packed.shape), PLANE), "c")
    return reduce(weight_parts(back, *tokens))


def solution(mesh):
    fine = Mesh(mesh.devices.reshape(NZ, NYH, NYL, NX, NC), AXES)
    dp, seq = ("z", "yh"), ("yl", "x", "c")
    placed = (P(dp, seq, None, None), P(dp, seq, None, None), P(seq, None))
    return jax.shard_map(shards, mesh=fine, in_specs=placed, out_specs=P(seq, None), check_vma=False)
```

```python
import functools
import itertools

import jax
import jax.numpy as jnp
from jax import lax
from jax.experimental import pallas as pl
from jax.experimental.pallas import tpu as pltpu
from jax.sharding import Mesh
from jax.sharding import PartitionSpec as P

NZ, NYH, NYL, NX, NC = 8, 2, 4, 4, 2
AXES = ("z", "yh", "yl", "x", "c")
BF = jnp.bfloat16
F32 = jnp.float32
VMEM = pl.BlockSpec(memory_space=pltpu.VMEM)
HBM = pl.BlockSpec(memory_space=pltpu.HBM)
LIMIT = 16 * 2**20


def device(z, yh, yl, x, c):
    return (((z * NYH + yh) * NYL + yl) * NX + x) * NC + c


def everyone():
    return itertools.product(range(NZ), range(NYH), range(NYL), range(NX), range(NC))


def groups(key, order):
    found = {}
    for at in everyone():
        found.setdefault(key(*at), []).append((order(*at), device(*at)))
    return [[d for _, d in sorted(members)] for members in found.values()]


def cube_groups(key, order):
    def named(names):
        def value(z, yh, yl, x, c):
            zs, ys, xs = (z + c) % NZ, (yh * NYL + yl + c) % (NYH * NYL), (x + c) % NX
            place = {"z1": zs // 2, "z0": zs % 2, "y2": ys // 4, "y1": ys // 2 % 2, "y0": ys % 2}
            place |= {"x1": xs // 2, "x0": xs % 2, "yl": yl, "x": x, "c": c}
            return tuple(place[name] for name in names)

        return value

    return groups(named(key), named(order))


LIGHT = cube_groups(("c", "z1", "z0", "y2", "y0", "x0"), ("y1", "x1"))
HEAVY = cube_groups(("c", "z1", "y2", "y1", "x1"), ("y0", "x0", "z0"))
SPREAD = cube_groups(("c", "y2", "y0", "x0", "z0"), ("y1", "x1", "z1"))
COPIES = cube_groups(("c", "yl", "x"), ("z1", "z0", "y2"))
PLANE = groups(
    lambda z, yh, yl, x, c: (z, yh, c),
    lambda z, yh, yl, x, c: ((yl + 1 + 2 * c) % NYL, (x + 2 * c) % NX),
)


def other_core(v):
    return lax.ppermute(v, "c", [(0, 1), (1, 0)])


def exchange(v, members):
    return lax.all_to_all(v, AXES, split_axis=0, concat_axis=0, axis_index_groups=members, tiled=True)


def half_shards():
    for yl, x, half in itertools.product(range(NYL), range(NX), range(2)):
        places = []
        for c in range(NC):
            ys, xs = (yl + c) % NYL, (x + c) % NX
            places.append((((ys % 2 * 2 + xs % 2) * 2 + half) * 2 + ys // 2) * 2 + xs // 2)
        yield yl, x, half, *places


def prepare_kernel(norm, value, own, away):
    c = lax.axis_index("c")
    width = value.shape[1]
    rows = width // (NYL * NX * NC)
    block = NX * NC * rows
    part = block // 2
    source = lax.broadcasted_iota(jnp.int32, (block, block), 0)
    k = lax.broadcasted_iota(jnp.int32, (block, block), 1)
    second = (k >= part).astype(jnp.int32)
    k = k - part * second
    wanted = k + rows * (second + c - 2 * c * second)
    for b in range(1, NX):
        wanted = wanted + rows * (k >= b * rows).astype(jnp.int32)
    pick = (source == wanted).astype(F32).astype(BF)
    if norm:
        wide = value[...].astype(F32)
        r = lax.rsqrt(jnp.mean(wide * wide, axis=-1, keepdims=True) + 1e-06)
    for a in range(NYL):
        tokens = value[:, a * block : (a + 1) * block]
        if norm:
            tokens = (tokens.astype(F32) * r).astype(BF)
        moved = jnp.dot(tokens, pick, preferred_element_type=F32).astype(BF)
        own[:, a * part : (a + 1) * part] = moved[:, :part]
        away[:, a * part : (a + 1) * part] = moved[:, part:]


def prepare(value, norm):
    tokens, width = value.shape
    shape = jax.ShapeDtypeStruct((tokens, width // 2), BF)
    return pl.pallas_call(
        functools.partial(prepare_kernel, norm),
        out_shape=(shape, shape),
        in_specs=[VMEM],
        out_specs=(VMEM, VMEM),
        compiler_params=pltpu.CompilerParams(vmem_limit_bytes=LIMIT),
        name="prepare",
    )(value)


def multiply(lat, cot, w, mine, theirs):
    c = lax.axis_index("c")
    head = w.shape[1] // 4
    count = lat.shape[0] // 2
    for tokens, at in ((lat, slice(0, 3 * head)), (cot, slice(3 * head, 4 * head))):
        value = jnp.dot(tokens[...], w[:, at], preferred_element_type=F32)
        to = (mine.shape[0], mine.shape[1], at.stop - at.start)
        low, high = value[:count], value[count:]
        mine[:, :, at] = jnp.where(c == 0, low, high).reshape(to)
        theirs[:, :, at] = jnp.where(c == 0, high, low).reshape(to).astype(BF)


def project_arrived_kernel(blocks, lat, cot, w, mine, theirs, keep_lat, keep_cot):
    c = lax.axis_index("c")
    keep_lat[...] = lat[...]
    keep_cot[...] = cot[...]
    rows = blocks.shape[1]
    for yl, x, half, even, odd in half_shards():
        place = (yl * NX + x) * 2 + half
        w[place * rows : (place + 1) * rows] = blocks[jnp.where(c == 0, even, odd)]
    multiply(lat, cot, w, mine, theirs)


def project_own_kernel(w, lat, cot, arr_mine, arr_theirs, mine, theirs, new_mine, new_theirs):
    c = lax.axis_index("c")
    multiply(lat, cot, w, new_mine, new_theirs)
    for old, new, to in ((arr_mine, new_mine, mine), (arr_theirs, new_theirs, theirs)):
        to[:, c] = new[...]
        to[:, 1 - c] = old[...]


def project(blocks, own_l, own_c, arr_l, arr_c):
    tokens, width = own_l.shape
    columns = blocks.shape[-1]
    chips = NYL * NX
    rows = tokens // (chips * NC)
    half, whole = (chips, rows, columns), (chips, NC, rows, columns)
    params = pltpu.CompilerParams(vmem_limit_bytes=LIMIT)
    w, mine, theirs, arr_l, arr_c = pl.pallas_call(
        project_arrived_kernel,
        out_shape=(
            jax.ShapeDtypeStruct((width, columns), BF),
            jax.ShapeDtypeStruct(half, F32),
            jax.ShapeDtypeStruct(half, BF),
            jax.ShapeDtypeStruct(arr_l.shape, BF),
            jax.ShapeDtypeStruct(arr_c.shape, BF),
        ),
        in_specs=[VMEM] * 3,
        out_specs=(VMEM,) * 5,
        compiler_params=params,
        name="project_arrived",
    )(blocks, arr_l, arr_c)
    mine, theirs = pl.pallas_call(
        project_own_kernel,
        out_shape=(jax.ShapeDtypeStruct(whole, F32), jax.ShapeDtypeStruct(whole, BF)),
        in_specs=[VMEM] * 5,
        out_specs=(VMEM,) * 2,
        scratch_shapes=[pltpu.VMEM(half, F32), pltpu.VMEM(half, BF)],
        compiler_params=params,
        name="project_own",
    )(w, own_l, own_c, mine, theirs)
    return mine, theirs, arr_l, arr_c


def weight_kernel(columns, back, own, arrived, *rest):
    blocks, grads = rest[-2:]
    c = lax.axis_index("c")
    _, chips, _, patches, _ = back.shape
    count = chips * patches
    rows = blocks.shape[1]
    source, to = columns
    for index, frame in ((0, c), (1, 1 - c)):
        for half in range(2):
            value = back[half, :, frame, :, source].astype(F32)
            grads[index, half * count : (half + 1) * count] = value.reshape(count, -1).astype(BF)
    wide = NX * 2 * rows
    for yl in range(NYL):
        part = slice(yl * wide, (yl + 1) * wide)
        value = 0.0
        for index, tokens in ((0, own), (1, arrived)):
            value = value + lax.dot_general(
                tokens[:, part], grads[index], (((0,), (0,)), ((), ())), preferred_element_type=F32
            )
        value = value.astype(BF)
        for y, x, half, even, odd in half_shards():
            if y == yl:
                piece = value[(x * 2 + half) * rows : (x * 2 + half + 1) * rows]
                blocks[jnp.where(c == 0, even, odd), :, to] = piece


def weight_parts(back, own_l, own_c, arr_l, arr_c):
    tokens, width = own_l.shape
    columns = back.shape[-1]
    head = columns // 4
    count = NYL * NX * 2

    def call(source, to, own, arrived, *blocks):
        return pl.pallas_call(
            functools.partial(weight_kernel, (source, to)),
            out_shape=jax.ShapeDtypeStruct((count, width // count, columns), BF),
            in_specs=[VMEM] * (3 + len(blocks)),
            out_specs=VMEM,
            scratch_shapes=[pltpu.VMEM((2, tokens, source.stop - source.start), BF)],
            input_output_aliases={3: 0} if blocks else {},
            compiler_params=pltpu.CompilerParams(vmem_limit_bytes=LIMIT),
            name="weight_parts",
        )(back, own, arrived, *blocks)

    blocks = call(slice(head, 4 * head), slice(0, 3 * head), own_l, arr_l)
    return call(slice(0, head), slice(3 * head, 4 * head), own_c, arr_c, blocks)


def attend_kernel(packed, result):
    tokens, columns = packed.shape
    head = columns // 4
    scale = 1.0 / head**0.5
    patches = tokens // (NYL * NX * NC)
    query, keys, values, grad_out = (packed[:, i * head : (i + 1) * head] for i in range(4))
    row = lax.broadcasted_iota(jnp.int32, (tokens, tokens), 0)
    column = lax.broadcasted_iota(jnp.int32, (tokens, tokens), 1)
    same = lax.rem(row, patches) == lax.rem(column, patches)
    across, down = (((1,), (1,)), ((), ())), (((0,), (0,)), ((), ()))
    scores = lax.dot_general(query, keys, across, preferred_element_type=F32) * scale
    scores = jnp.where(same, scores, -jnp.inf)
    weights = jnp.exp(scores - jnp.max(scores, axis=-1, keepdims=True))
    probs = weights / jnp.sum(weights, axis=-1, keepdims=True)
    probs_b = probs.astype(BF)
    out = jnp.dot(probs_b, values, preferred_element_type=F32).astype(BF)
    result[:, :head] = out
    grad_v = lax.dot_general(probs_b, grad_out, down, preferred_element_type=F32)
    result[:, 3 * head :] = grad_v.astype(BF)
    grad_probs = lax.dot_general(grad_out, values, across, preferred_element_type=F32)
    delta = jnp.sum(grad_out.astype(F32) * out.astype(F32), axis=-1, keepdims=True)
    grad_scores = jnp.where(same, probs * (grad_probs - delta), 0.0).astype(BF)
    grad_q = jnp.dot(grad_scores, keys, preferred_element_type=F32) * scale
    result[:, head : 2 * head] = grad_q.astype(BF)
    grad_k = lax.dot_general(grad_scores, query, down, preferred_element_type=F32) * scale
    result[:, 2 * head : 3 * head] = grad_k.astype(BF)


def attend(packed):
    return pl.pallas_call(
        attend_kernel,
        out_shape=jax.ShapeDtypeStruct(packed.shape, BF),
        in_specs=[VMEM],
        out_specs=VMEM,
        compiler_params=pltpu.CompilerParams(vmem_limit_bytes=LIMIT),
        name="attend",
    )(packed)


def repeat_kernel(value, copies, sems):
    started = [pltpu.make_async_copy(value, copies.at[i], sems.at[i]) for i in range(copies.shape[0])]
    for copy in started:
        copy.start()
    for copy in started:
        copy.wait()


def repeat(value, count):
    return pl.pallas_call(
        repeat_kernel,
        out_shape=jax.ShapeDtypeStruct((count, *value.shape), value.dtype),
        in_specs=[VMEM],
        out_specs=HBM,
        scratch_shapes=[pltpu.SemaphoreType.DMA((count,))],
        compiler_params=pltpu.CompilerParams(vmem_limit_bytes=LIMIT),
        name="repeat",
    )(value)


def finish_kernel(copies, total):
    _, _, rows, columns = copies.shape
    for z1, z0 in itertools.product(range(NZ // 2), range(2)):
        index = z1 * 2 + z0
        value = copies[index, 0].astype(F32) + copies[index, 1].astype(F32)
        total[z0 * rows : (z0 + 1) * rows, z1 * columns : (z1 + 1) * columns] = value


def finish(copies):
    _, _, rows, columns = copies.shape
    return pl.pallas_call(
        finish_kernel,
        out_shape=jax.ShapeDtypeStruct((2 * rows, NZ // 2 * columns), F32),
        in_specs=[VMEM],
        out_specs=VMEM,
        compiler_params=pltpu.CompilerParams(vmem_limit_bytes=LIMIT),
        name="finish",
    )(copies)


def gather(weights, own):
    rows, columns = weights.shape
    z0 = lax.rem(lax.axis_index("z") + lax.axis_index("c"), 2)
    half = lax.dynamic_slice_in_dim(weights, z0 * (rows // 2), rows // 2)
    four = exchange(jnp.broadcast_to(half[None], (4, rows // 2, columns)), LIGHT)
    four, own = lax.optimization_barrier((four, own))
    blocks = exchange(repeat(four, 8), HEAVY)
    return blocks.reshape(32, rows // 2, columns), own


def reduce(blocks):
    _, rows, columns = blocks.shape
    heavy = exchange(blocks.reshape(8, 4, rows, columns), HEAVY)
    four = jnp.sum(heavy.astype(F32), axis=0).astype(BF)
    pieces = four.reshape(4, rows, 4, columns // 4).transpose(0, 2, 1, 3).reshape(16, rows, columns // 4)
    piece = jnp.sum(exchange(pieces, SPREAD).astype(F32), axis=0).astype(BF)
    copies = exchange(jnp.broadcast_to(piece[None], (NZ * NYH, *piece.shape)), COPIES)
    return finish(copies.reshape(NZ, NYH, *piece.shape))


def shards(latents, cotangent, weights):
    width = latents.shape[-1]
    columns = weights.shape[1]
    own_l, away_l = prepare(latents.reshape(-1, width), True)
    own_c, away_c = prepare(cotangent.reshape(-1, width), False)
    blocks, own_l = gather(weights, own_l)
    tokens = own_l, own_c, other_core(away_l), other_core(away_c)
    mine, theirs, *arrived = project(blocks, *tokens)
    tokens = *tokens[:2], *arrived
    both = lax.all_gather(theirs, "c")
    part = lax.dynamic_index_in_dim(both, 1 - lax.axis_index("c"), keepdims=False)
    packed = exchange((mine + part.astype(F32)).astype(BF), PLANE)
    result = attend(packed.reshape(-1, columns))
    back = lax.all_gather(exchange(result.reshape(packed.shape), PLANE), "c")
    return reduce(weight_parts(back, *tokens))


def solution(mesh):
    fine = Mesh(mesh.devices.reshape(NZ, NYH, NYL, NX, NC), AXES)
    dp, seq = ("z", "yh"), ("yl", "x", "c")
    placed = (P(dp, seq, None, None), P(dp, seq, None, None), P(seq, None))
    return jax.shard_map(shards, mesh=fine, in_specs=placed, out_specs=P(seq, None), check_vma=False)
```

```python
import functools
import itertools

import jax
import jax.numpy as jnp
from jax import lax
from jax.experimental import pallas as pl
from jax.experimental.pallas import tpu as pltpu
from jax.sharding import Mesh
from jax.sharding import PartitionSpec as P

NZ, NYH, NYL, NX, NC = 8, 2, 4, 4, 2
AXES = ("z", "yh", "yl", "x", "c")
BF = jnp.bfloat16
F32 = jnp.float32
VMEM = pl.BlockSpec(memory_space=pltpu.VMEM)
HBM = pl.BlockSpec(memory_space=pltpu.HBM)
LIMIT = 16 * 2**20


def device(z, yh, yl, x, c):
    return (((z * NYH + yh) * NYL + yl) * NX + x) * NC + c


def everyone():
    return itertools.product(range(NZ), range(NYH), range(NYL), range(NX), range(NC))


def groups(key, order):
    found = {}
    for at in everyone():
        found.setdefault(key(*at), []).append((order(*at), device(*at)))
    return [[d for _, d in sorted(members)] for members in found.values()]


def cube_groups(key, order):
    def named(names):
        def value(z, yh, yl, x, c):
            zs, ys, xs = (z + c) % NZ, (yh * NYL + yl + c) % (NYH * NYL), (x + c) % NX
            place = {"z1": zs // 2, "z0": zs % 2, "y2": ys // 4, "y1": ys // 2 % 2, "y0": ys % 2}
            place |= {"x1": xs // 2, "x0": xs % 2, "yl": yl, "x": x, "c": c}
            return tuple(place[name] for name in names)

        return value

    return groups(named(key), named(order))


LIGHT = cube_groups(("c", "z1", "z0", "y2", "y0", "x0"), ("y1", "x1"))
HEAVY = cube_groups(("c", "z1", "y2", "y1", "x1"), ("y0", "x0", "z0"))
SPREAD = cube_groups(("c", "y2", "y0", "x0", "z0"), ("y1", "x1", "z1"))
COPIES = cube_groups(("c", "yl", "x"), ("z1", "z0", "y2"))
PLANE = groups(
    lambda z, yh, yl, x, c: (z, yh, c),
    lambda z, yh, yl, x, c: ((yl + 1 + 2 * c) % NYL, (x + 2 * c) % NX),
)


def other_core(v):
    return lax.ppermute(v, "c", [(0, 1), (1, 0)])


def exchange(v, members):
    return lax.all_to_all(v, AXES, split_axis=0, concat_axis=0, axis_index_groups=members, tiled=True)


def half_shards():
    for yl, x, half in itertools.product(range(NYL), range(NX), range(2)):
        places = []
        for c in range(NC):
            ys, xs = (yl + c) % NYL, (x + c) % NX
            places.append((((ys % 2 * 2 + xs % 2) * 2 + half) * 2 + ys // 2) * 2 + xs // 2)
        yield yl, x, half, *places


def prepare_kernel(lat, cot, own_l, own_c, away):
    c = lax.axis_index("c")
    width = lat.shape[1]
    rows = width // (NYL * NX * NC)
    block = NX * NC * rows
    part = block // 2
    source = lax.broadcasted_iota(jnp.int32, (block, block), 0)
    k = lax.broadcasted_iota(jnp.int32, (block, block), 1)
    second = (k >= part).astype(jnp.int32)
    k = k - part * second
    wanted = k + rows * (second + c - 2 * c * second)
    for b in range(1, NX):
        wanted = wanted + rows * (k >= b * rows).astype(jnp.int32)
    pick = (source == wanted).astype(F32).astype(BF)
    wide = lat[...].astype(F32)
    r = lax.rsqrt(jnp.mean(wide * wide, axis=-1, keepdims=True) + 1e-06)
    for a in range(NYL):
        at, to = slice(a * block, (a + 1) * block), slice(a * part, (a + 1) * part)
        normed = (lat[:, at].astype(F32) * r).astype(BF)
        for index, own, tokens in ((0, own_l, normed), (1, own_c, cot[:, at])):
            moved = jnp.dot(tokens, pick, preferred_element_type=F32).astype(BF)
            own[:, to] = moved[:, :part]
            away[index, :, to] = moved[:, part:]


def prepare(lat, cot):
    tokens, width = lat.shape
    shape = tokens, width // 2
    one = jax.ShapeDtypeStruct(shape, BF)
    return pl.pallas_call(
        prepare_kernel,
        out_shape=(one, one, jax.ShapeDtypeStruct((2, *shape), BF)),
        in_specs=[VMEM] * 2,
        out_specs=(VMEM,) * 3,
        compiler_params=pltpu.CompilerParams(vmem_limit_bytes=LIMIT),
        name="prepare",
    )(lat, cot)


def project_kernel(blocks, own_l, own_c, arrived, mine, theirs, keep, w):
    c = lax.axis_index("c")
    rows = blocks.shape[1]
    for yl, x, half, even, odd in half_shards():
        place = (yl * NX + x) * 2 + half
        w[place * rows : (place + 1) * rows] = blocks[jnp.where(c == 0, even, odd)]
    head = w.shape[1] // 4
    count = own_l.shape[0] // 2
    for frame, lat, cot in ((c, own_l, own_c), (1 - c, arrived.at[0], arrived.at[1])):
        for tokens, at in ((lat, slice(0, 3 * head)), (cot, slice(3 * head, 4 * head))):
            value = jnp.dot(tokens[...], w[:, at], preferred_element_type=F32)
            to = (mine.shape[0], mine.shape[2], at.stop - at.start)
            low, high = value[:count], value[count:]
            mine[:, frame, :, at] = jnp.where(c == 0, low, high).reshape(to)
            theirs[:, frame, :, at] = jnp.where(c == 0, high, low).reshape(to).astype(BF)
    keep[...] = arrived[...]


def project(blocks, own_l, own_c, arrived):
    tokens, width = own_l.shape
    columns = blocks.shape[-1]
    chips = NYL * NX
    shape = (chips, NC, tokens // (chips * NC), columns)
    kept = jax.ShapeDtypeStruct(arrived.shape, BF)
    return pl.pallas_call(
        project_kernel,
        out_shape=(jax.ShapeDtypeStruct(shape, F32), jax.ShapeDtypeStruct(shape, BF), kept),
        in_specs=[VMEM] * 4,
        out_specs=(VMEM,) * 3,
        scratch_shapes=[pltpu.VMEM((width, columns), BF)],
        compiler_params=pltpu.CompilerParams(vmem_limit_bytes=LIMIT),
        name="project",
    )(blocks, own_l, own_c, arrived)


def weight_kernel(back, own_l, own_c, arrived, blocks, grads):
    c = lax.axis_index("c")
    _, chips, _, patches, columns = back.shape
    head = columns // 4
    count = chips * patches
    rows = blocks.shape[1]
    for index, frame in ((0, c), (1, 1 - c)):
        for half in range(2):
            value = back[half, :, frame].astype(F32).reshape(count, columns)
            grads[index, half * count : (half + 1) * count] = value.astype(BF)
    wide = NX * 2 * rows

    def multiply(own, arrived, at, to):
        for yl in range(NYL):
            part = slice(yl * wide, (yl + 1) * wide)
            value = 0.0
            for index, tokens in ((0, own), (1, arrived)):
                value = value + lax.dot_general(
                    tokens[:, part],
                    grads[index, :, at],
                    (((0,), (0,)), ((), ())),
                    preferred_element_type=F32,
                )
            value = value.astype(BF)
            for y, x, half, even, odd in half_shards():
                if y == yl:
                    piece = value[(x * 2 + half) * rows : (x * 2 + half + 1) * rows]
                    blocks[jnp.where(c == 0, even, odd), :, to] = piece

    multiply(own_l, arrived.at[0], slice(head, 4 * head), slice(0, 3 * head))
    multiply(own_c, arrived.at[1], slice(0, head), slice(3 * head, 4 * head))


def weight_parts(back, own_l, own_c, arrived):
    tokens, width = own_l.shape
    columns = back.shape[-1]
    count = NYL * NX * 2
    return pl.pallas_call(
        weight_kernel,
        out_shape=jax.ShapeDtypeStruct((count, width // count, columns), BF),
        in_specs=[VMEM] * 4,
        out_specs=VMEM,
        scratch_shapes=[pltpu.VMEM((2, tokens, columns), BF)],
        compiler_params=pltpu.CompilerParams(vmem_limit_bytes=LIMIT),
        name="weight_parts",
    )(back, own_l, own_c, arrived)


def attend_kernel(packed, result):
    tokens, columns = packed.shape
    head = columns // 4
    scale = 1.0 / head**0.5
    patches = tokens // (NYL * NX * NC)
    query, keys, values, grad_out = (packed[:, i * head : (i + 1) * head] for i in range(4))
    row = lax.broadcasted_iota(jnp.int32, (tokens, tokens), 0)
    column = lax.broadcasted_iota(jnp.int32, (tokens, tokens), 1)
    same = lax.rem(row, patches) == lax.rem(column, patches)
    across, down = (((1,), (1,)), ((), ())), (((0,), (0,)), ((), ()))
    scores = lax.dot_general(query, keys, across, preferred_element_type=F32) * scale
    scores = jnp.where(same, scores, -jnp.inf)
    weights = jnp.exp(scores - jnp.max(scores, axis=-1, keepdims=True))
    probs = weights / jnp.sum(weights, axis=-1, keepdims=True)
    probs_b = probs.astype(BF)
    out = jnp.dot(probs_b, values, preferred_element_type=F32).astype(BF)
    result[:, :head] = out
    grad_v = lax.dot_general(probs_b, grad_out, down, preferred_element_type=F32)
    result[:, 3 * head :] = grad_v.astype(BF)
    grad_probs = lax.dot_general(grad_out, values, across, preferred_element_type=F32)
    delta = jnp.sum(grad_out.astype(F32) * out.astype(F32), axis=-1, keepdims=True)
    grad_scores = jnp.where(same, probs * (grad_probs - delta), 0.0).astype(BF)
    grad_q = jnp.dot(grad_scores, keys, preferred_element_type=F32) * scale
    result[:, head : 2 * head] = grad_q.astype(BF)
    grad_k = lax.dot_general(grad_scores, query, down, preferred_element_type=F32) * scale
    result[:, 2 * head : 3 * head] = grad_k.astype(BF)


def attend(packed):
    return pl.pallas_call(
        attend_kernel,
        out_shape=jax.ShapeDtypeStruct(packed.shape, BF),
        in_specs=[VMEM],
        out_specs=VMEM,
        compiler_params=pltpu.CompilerParams(vmem_limit_bytes=LIMIT),
        name="attend",
    )(packed)


def repeat_kernel(value, copies, sems):
    started = [pltpu.make_async_copy(value, copies.at[i], sems.at[i]) for i in range(copies.shape[0])]
    for copy in started:
        copy.start()
    for copy in started:
        copy.wait()


def repeat(value, count):
    return pl.pallas_call(
        repeat_kernel,
        out_shape=jax.ShapeDtypeStruct((count, *value.shape), value.dtype),
        in_specs=[VMEM],
        out_specs=HBM,
        scratch_shapes=[pltpu.SemaphoreType.DMA((count,))],
        compiler_params=pltpu.CompilerParams(vmem_limit_bytes=LIMIT),
        name="repeat",
    )(value)


def finish_kernel(copies, total):
    _, _, rows, columns = copies.shape
    for z1, z0 in itertools.product(range(NZ // 2), range(2)):
        index = z1 * 2 + z0
        value = copies[index, 0].astype(F32) + copies[index, 1].astype(F32)
        total[z0 * rows : (z0 + 1) * rows, z1 * columns : (z1 + 1) * columns] = value


def finish(copies):
    _, _, rows, columns = copies.shape
    return pl.pallas_call(
        finish_kernel,
        out_shape=jax.ShapeDtypeStruct((2 * rows, NZ // 2 * columns), F32),
        in_specs=[VMEM],
        out_specs=VMEM,
        compiler_params=pltpu.CompilerParams(vmem_limit_bytes=LIMIT),
        name="finish",
    )(copies)


def gather(weights, own):
    rows, columns = weights.shape
    z0 = lax.rem(lax.axis_index("z") + lax.axis_index("c"), 2)
    half = lax.dynamic_slice_in_dim(weights, z0 * (rows // 2), rows // 2)
    four = exchange(jnp.broadcast_to(half[None], (4, rows // 2, columns)), LIGHT)
    four, own = lax.optimization_barrier((four, own))
    blocks = exchange(repeat(four, 8), HEAVY)
    return blocks.reshape(32, rows // 2, columns), own


def reduce(blocks):
    _, rows, columns = blocks.shape
    heavy = exchange(blocks.reshape(8, 4, rows, columns), HEAVY)
    four = jnp.sum(heavy.astype(F32), axis=0).astype(BF)
    pieces = four.reshape(4, rows, 4, columns // 4).transpose(0, 2, 1, 3).reshape(16, rows, columns // 4)
    piece = jnp.sum(exchange(pieces, SPREAD).astype(F32), axis=0).astype(BF)
    copies = exchange(jnp.broadcast_to(piece[None], (NZ * NYH, *piece.shape)), COPIES)
    return finish(copies.reshape(NZ, NYH, *piece.shape))


def shards(latents, cotangent, weights):
    width = latents.shape[-1]
    columns = weights.shape[1]
    own_l, own_c, away = prepare(latents.reshape(-1, width), cotangent.reshape(-1, width))
    blocks, own_l = gather(weights, own_l)
    mine, theirs, arrived = project(blocks, own_l, own_c, other_core(away))
    tokens = own_l, own_c, arrived
    both = lax.all_gather(theirs, "c")
    part = lax.dynamic_index_in_dim(both, 1 - lax.axis_index("c"), keepdims=False)
    packed = exchange((mine + part.astype(F32)).astype(BF), PLANE)
    result = attend(packed.reshape(-1, columns))
    back = lax.all_gather(exchange(result.reshape(packed.shape), PLANE), "c")
    return reduce(weight_parts(back, *tokens))


def solution(mesh):
    fine = Mesh(mesh.devices.reshape(NZ, NYH, NYL, NX, NC), AXES)
    dp, seq = ("z", "yh"), ("yl", "x", "c")
    placed = (P(dp, seq, None, None), P(dp, seq, None, None), P(seq, None))
    return jax.shard_map(shards, mesh=fine, in_specs=placed, out_specs=P(seq, None), check_vma=False)
```

```python
import functools
import itertools

import jax
import jax.numpy as jnp
from jax import lax
from jax.experimental import pallas as pl
from jax.experimental.pallas import tpu as pltpu
from jax.sharding import Mesh
from jax.sharding import PartitionSpec as P

NZ, NYH, NYL, NX, NC = 8, 2, 4, 4, 2
AXES = ("z", "yh", "yl", "x", "c")
BF = jnp.bfloat16
F32 = jnp.float32
VMEM = pl.BlockSpec(memory_space=pltpu.VMEM)
HBM = pl.BlockSpec(memory_space=pltpu.HBM)
LIMIT = 16 * 2**20


def device(z, yh, yl, x, c):
    return (((z * NYH + yh) * NYL + yl) * NX + x) * NC + c


def everyone():
    return itertools.product(range(NZ), range(NYH), range(NYL), range(NX), range(NC))


def groups(key, order):
    found = {}
    for at in everyone():
        found.setdefault(key(*at), []).append((order(*at), device(*at)))
    return [[d for _, d in sorted(members)] for members in found.values()]


def cube_groups(key, order):
    def named(names):
        def value(z, yh, yl, x, c):
            zs, ys, xs = (z + c) % NZ, (yh * NYL + yl + c) % (NYH * NYL), (x + c) % NX
            place = {"z1": zs // 2, "z0": zs % 2, "y2": ys // 4, "y1": ys // 2 % 2, "y0": ys % 2}
            place |= {"x1": xs // 2, "x0": xs % 2, "yl": yl, "x": x, "c": c}
            return tuple(place[name] for name in names)

        return value

    return groups(named(key), named(order))


LIGHT = cube_groups(("c", "z1", "z0", "y2", "y0", "x0"), ("y1", "x1"))
HEAVY = cube_groups(("c", "z1", "y2", "y1", "x1"), ("y0", "x0", "z0"))
SPREAD = cube_groups(("c", "y2", "y0", "x0", "z0"), ("y1", "x1", "z1"))
COPIES = cube_groups(("c", "yl", "x"), ("z1", "z0", "y2"))
PLANE = groups(
    lambda z, yh, yl, x, c: (z, yh, c),
    lambda z, yh, yl, x, c: ((yl + 1 + 2 * c) % NYL, (x + 2 * c) % NX),
)


def other_core(v):
    return lax.ppermute(v, "c", [(0, 1), (1, 0)])


def exchange(v, members):
    return lax.all_to_all(v, AXES, split_axis=0, concat_axis=0, axis_index_groups=members, tiled=True)


def half_shards():
    for yl, x, half in itertools.product(range(NYL), range(NX), range(2)):
        places = []
        for c in range(NC):
            ys, xs = (yl + c) % NYL, (x + c) % NX
            places.append((((ys % 2 * 2 + xs % 2) * 2 + half) * 2 + ys // 2) * 2 + xs // 2)
        yield yl, x, half, *places


def prepare_kernel(lat, cot, own_l, own_c, away):
    c = lax.axis_index("c")
    width = lat.shape[1]
    rows = width // (NYL * NX * NC)
    block = NX * NC * rows
    part = block // 2
    source = lax.broadcasted_iota(jnp.int32, (part, part), 0)
    k = lax.broadcasted_iota(jnp.int32, (part, part), 1)
    second = (k >= part // 2).astype(jnp.int32)
    k = k - part // 2 * second
    k = k + rows * (k >= rows).astype(jnp.int32)
    parity = second + c - 2 * c * second
    low = (source == k + rows * parity).astype(F32).astype(BF)
    high = (source == k + rows * (1 - parity)).astype(F32).astype(BF)
    first = lax.broadcasted_iota(jnp.int32, (lat.shape[0], part), 1) < part // 2
    wide = lat[...].astype(F32)
    r = lax.rsqrt(jnp.mean(wide * wide, axis=-1, keepdims=True) + 1e-06)
    for a in range(NYL):
        at, to = slice(a * block, (a + 1) * block), slice(a * part, (a + 1) * part)
        normed = (lat[:, at].astype(F32) * r).astype(BF)
        for index, own, tokens in ((0, own_l, normed), (1, own_c, cot[:, at])):
            one = jnp.dot(tokens[:, :part], low, preferred_element_type=F32)
            two = jnp.dot(tokens[:, part:], high, preferred_element_type=F32)
            own[:, to] = jnp.where(first, one, two).astype(BF)
            away[index, :, to] = pltpu.roll(jnp.where(first, two, one), part // 2, 1).astype(BF)


def prepare(lat, cot):
    tokens, width = lat.shape
    shape = tokens, width // 2
    one = jax.ShapeDtypeStruct(shape, BF)
    return pl.pallas_call(
        prepare_kernel,
        out_shape=(one, one, jax.ShapeDtypeStruct((2, *shape), BF)),
        in_specs=[VMEM] * 2,
        out_specs=(VMEM,) * 3,
        compiler_params=pltpu.CompilerParams(vmem_limit_bytes=LIMIT),
        name="prepare",
    )(lat, cot)


def project_kernel(blocks, own_l, own_c, arrived, mine, theirs, keep, w):
    c = lax.axis_index("c")
    rows = blocks.shape[1]
    for yl, x, half, even, odd in half_shards():
        place = (yl * NX + x) * 2 + half
        w[place * rows : (place + 1) * rows] = blocks[jnp.where(c == 0, even, odd)]
    head = w.shape[1] // 4
    count = own_l.shape[0] // 2
    for frame, lat, cot in ((c, own_l, own_c), (1 - c, arrived.at[0], arrived.at[1])):
        for tokens, at in ((lat, slice(0, 3 * head)), (cot, slice(3 * head, 4 * head))):
            value = jnp.dot(tokens[...], w[:, at], preferred_element_type=F32)
            to = (mine.shape[0], mine.shape[2], at.stop - at.start)
            low, high = value[:count], value[count:]
            mine[:, frame, :, at] = jnp.where(c == 0, low, high).reshape(to)
            theirs[:, frame, :, at] = jnp.where(c == 0, high, low).reshape(to).astype(BF)
    keep[...] = arrived[...]


def project(blocks, own_l, own_c, arrived):
    tokens, width = own_l.shape
    columns = blocks.shape[-1]
    chips = NYL * NX
    shape = (chips, NC, tokens // (chips * NC), columns)
    kept = jax.ShapeDtypeStruct(arrived.shape, BF)
    return pl.pallas_call(
        project_kernel,
        out_shape=(jax.ShapeDtypeStruct(shape, F32), jax.ShapeDtypeStruct(shape, BF), kept),
        in_specs=[VMEM] * 4,
        out_specs=(VMEM,) * 3,
        scratch_shapes=[pltpu.VMEM((width, columns), BF)],
        compiler_params=pltpu.CompilerParams(vmem_limit_bytes=LIMIT),
        name="project",
    )(blocks, own_l, own_c, arrived)


def weight_kernel(back, own_l, own_c, arrived, blocks, grads):
    c = lax.axis_index("c")
    _, chips, _, patches, columns = back.shape
    head = columns // 4
    count = chips * patches
    rows = blocks.shape[1]
    for index, frame in ((0, c), (1, 1 - c)):
        for half in range(2):
            value = back[half, :, frame].astype(F32).reshape(count, columns)
            grads[index, half * count : (half + 1) * count] = value.astype(BF)
    wide = NX * 2 * rows

    def multiply(own, arrived, at, to):
        for yl in range(NYL):
            part = slice(yl * wide, (yl + 1) * wide)
            value = 0.0
            for index, tokens in ((0, own), (1, arrived)):
                value = value + lax.dot_general(
                    tokens[:, part],
                    grads[index, :, at],
                    (((0,), (0,)), ((), ())),
                    preferred_element_type=F32,
                )
            value = value.astype(BF)
            for y, x, half, even, odd in half_shards():
                if y == yl:
                    piece = value[(x * 2 + half) * rows : (x * 2 + half + 1) * rows]
                    blocks[jnp.where(c == 0, even, odd), :, to] = piece

    multiply(own_l, arrived.at[0], slice(head, 4 * head), slice(0, 3 * head))
    multiply(own_c, arrived.at[1], slice(0, head), slice(3 * head, 4 * head))


def weight_parts(back, own_l, own_c, arrived):
    tokens, width = own_l.shape
    columns = back.shape[-1]
    count = NYL * NX * 2
    return pl.pallas_call(
        weight_kernel,
        out_shape=jax.ShapeDtypeStruct((count, width // count, columns), BF),
        in_specs=[VMEM] * 4,
        out_specs=VMEM,
        scratch_shapes=[pltpu.VMEM((2, tokens, columns), BF)],
        compiler_params=pltpu.CompilerParams(vmem_limit_bytes=LIMIT),
        name="weight_parts",
    )(back, own_l, own_c, arrived)


def attend_kernel(packed, result):
    tokens, columns = packed.shape
    head = columns // 4
    scale = 1.0 / head**0.5
    patches = tokens // (NYL * NX * NC)
    query, keys, values, grad_out = (packed[:, i * head : (i + 1) * head] for i in range(4))
    row = lax.broadcasted_iota(jnp.int32, (tokens, tokens), 0)
    column = lax.broadcasted_iota(jnp.int32, (tokens, tokens), 1)
    same = lax.rem(row, patches) == lax.rem(column, patches)
    across, down = (((1,), (1,)), ((), ())), (((0,), (0,)), ((), ()))
    scores = lax.dot_general(query, keys, across, preferred_element_type=F32) * scale
    scores = jnp.where(same, scores, -jnp.inf)
    weights = jnp.exp(scores - jnp.max(scores, axis=-1, keepdims=True))
    probs = weights / jnp.sum(weights, axis=-1, keepdims=True)
    probs_b = probs.astype(BF)
    out = jnp.dot(probs_b, values, preferred_element_type=F32).astype(BF)
    result[:, :head] = out
    grad_v = lax.dot_general(probs_b, grad_out, down, preferred_element_type=F32)
    result[:, 3 * head :] = grad_v.astype(BF)
    grad_probs = lax.dot_general(grad_out, values, across, preferred_element_type=F32)
    delta = jnp.sum(grad_out.astype(F32) * out.astype(F32), axis=-1, keepdims=True)
    grad_scores = jnp.where(same, probs * (grad_probs - delta), 0.0).astype(BF)
    grad_q = jnp.dot(grad_scores, keys, preferred_element_type=F32) * scale
    result[:, head : 2 * head] = grad_q.astype(BF)
    grad_k = lax.dot_general(grad_scores, query, down, preferred_element_type=F32) * scale
    result[:, 2 * head : 3 * head] = grad_k.astype(BF)


def attend(packed):
    return pl.pallas_call(
        attend_kernel,
        out_shape=jax.ShapeDtypeStruct(packed.shape, BF),
        in_specs=[VMEM],
        out_specs=VMEM,
        compiler_params=pltpu.CompilerParams(vmem_limit_bytes=LIMIT),
        name="attend",
    )(packed)


def repeat_kernel(value, copies, sems):
    started = [pltpu.make_async_copy(value, copies.at[i], sems.at[i]) for i in range(copies.shape[0])]
    for copy in started:
        copy.start()
    for copy in started:
        copy.wait()


def repeat(value, count):
    return pl.pallas_call(
        repeat_kernel,
        out_shape=jax.ShapeDtypeStruct((count, *value.shape), value.dtype),
        in_specs=[VMEM],
        out_specs=HBM,
        scratch_shapes=[pltpu.SemaphoreType.DMA((count,))],
        compiler_params=pltpu.CompilerParams(vmem_limit_bytes=LIMIT),
        name="repeat",
    )(value)


def finish_kernel(copies, total):
    _, _, rows, columns = copies.shape
    for z1, z0 in itertools.product(range(NZ // 2), range(2)):
        index = z1 * 2 + z0
        value = copies[index, 0].astype(F32) + copies[index, 1].astype(F32)
        total[z0 * rows : (z0 + 1) * rows, z1 * columns : (z1 + 1) * columns] = value


def finish(copies):
    _, _, rows, columns = copies.shape
    return pl.pallas_call(
        finish_kernel,
        out_shape=jax.ShapeDtypeStruct((2 * rows, NZ // 2 * columns), F32),
        in_specs=[VMEM],
        out_specs=VMEM,
        compiler_params=pltpu.CompilerParams(vmem_limit_bytes=LIMIT),
        name="finish",
    )(copies)


def gather(weights, own):
    rows, columns = weights.shape
    z0 = lax.rem(lax.axis_index("z") + lax.axis_index("c"), 2)
    half = lax.dynamic_slice_in_dim(weights, z0 * (rows // 2), rows // 2)
    four = exchange(jnp.broadcast_to(half[None], (4, rows // 2, columns)), LIGHT)
    four, own = lax.optimization_barrier((four, own))
    blocks = exchange(repeat(four, 8), HEAVY)
    return blocks.reshape(32, rows // 2, columns), own


def reduce(blocks):
    _, rows, columns = blocks.shape
    heavy = exchange(blocks.reshape(8, 4, rows, columns), HEAVY)
    four = jnp.sum(heavy.astype(F32), axis=0).astype(BF)
    pieces = four.reshape(4, rows, 4, columns // 4).transpose(0, 2, 1, 3).reshape(16, rows, columns // 4)
    piece = jnp.sum(exchange(pieces, SPREAD).astype(F32), axis=0).astype(BF)
    copies = exchange(jnp.broadcast_to(piece[None], (NZ * NYH, *piece.shape)), COPIES)
    return finish(copies.reshape(NZ, NYH, *piece.shape))


def shards(latents, cotangent, weights):
    width = latents.shape[-1]
    columns = weights.shape[1]
    own_l, own_c, away = prepare(latents.reshape(-1, width), cotangent.reshape(-1, width))
    blocks, own_l = gather(weights, own_l)
    mine, theirs, arrived = project(blocks, own_l, own_c, other_core(away))
    tokens = own_l, own_c, arrived
    both = lax.all_gather(theirs, "c")
    part = lax.dynamic_index_in_dim(both, 1 - lax.axis_index("c"), keepdims=False)
    packed = exchange((mine + part.astype(F32)).astype(BF), PLANE)
    result = attend(packed.reshape(-1, columns))
    back = lax.all_gather(exchange(result.reshape(packed.shape), PLANE), "c")
    return reduce(weight_parts(back, *tokens))


def solution(mesh):
    fine = Mesh(mesh.devices.reshape(NZ, NYH, NYL, NX, NC), AXES)
    dp, seq = ("z", "yh"), ("yl", "x", "c")
    placed = (P(dp, seq, None, None), P(dp, seq, None, None), P(seq, None))
    return jax.shard_map(shards, mesh=fine, in_specs=placed, out_specs=P(seq, None), check_vma=False)
```

```python
import functools
import itertools

import jax
import jax.numpy as jnp
from jax import lax
from jax.experimental import pallas as pl
from jax.experimental.pallas import tpu as pltpu
from jax.sharding import Mesh
from jax.sharding import PartitionSpec as P

NZ, NYH, NYL, NX, NC = 8, 2, 4, 4, 2
AXES = ("z", "yh", "yl", "x", "c")
BF = jnp.bfloat16
F32 = jnp.float32
VMEM = pl.BlockSpec(memory_space=pltpu.VMEM)
HBM = pl.BlockSpec(memory_space=pltpu.HBM)
LIMIT = 16 * 2**20


def device(z, yh, yl, x, c):
    return (((z * NYH + yh) * NYL + yl) * NX + x) * NC + c


def everyone():
    return itertools.product(range(NZ), range(NYH), range(NYL), range(NX), range(NC))


def groups(key, order):
    found = {}
    for at in everyone():
        found.setdefault(key(*at), []).append((order(*at), device(*at)))
    return [[d for _, d in sorted(members)] for members in found.values()]


def cube_groups(key, order):
    def named(names):
        def value(z, yh, yl, x, c):
            zs, ys, xs = (z + c) % NZ, (yh * NYL + yl + c) % (NYH * NYL), (x + c) % NX
            place = {"z1": zs // 2, "z0": zs % 2, "y2": ys // 4, "y1": ys // 2 % 2, "y0": ys % 2}
            place |= {"x1": xs // 2, "x0": xs % 2, "yl": yl, "x": x, "c": c}
            return tuple(place[name] for name in names)

        return value

    return groups(named(key), named(order))


LIGHT = cube_groups(("c", "z1", "z0", "y2", "y0", "x0"), ("y1", "x1"))
HEAVY = cube_groups(("c", "z1", "y2", "y1", "x1"), ("y0", "x0", "z0"))
SPREAD = cube_groups(("c", "y2", "y0", "x0", "z0"), ("y1", "x1", "z1"))
COPIES = cube_groups(("c", "yl", "x"), ("z1", "z0", "y2"))
PLANE = groups(
    lambda z, yh, yl, x, c: (z, yh, c),
    lambda z, yh, yl, x, c: ((yl + 1 + 2 * c) % NYL, (x + 2 * c) % NX),
)


def other_core(v):
    return lax.ppermute(v, "c", [(0, 1), (1, 0)])


def exchange(v, members):
    return lax.all_to_all(v, AXES, split_axis=0, concat_axis=0, axis_index_groups=members, tiled=True)


def half_shards():
    for yl, x, half in itertools.product(range(NYL), range(NX), range(2)):
        places = []
        for c in range(NC):
            ys, xs = (yl + c) % NYL, (x + c) % NX
            places.append((((ys % 2 * 2 + xs % 2) * 2 + half) * 2 + ys // 2) * 2 + xs // 2)
        yield yl, x, half, *places


def prepare_kernel(norm, value, own, away):
    c = lax.axis_index("c")
    width = value.shape[1]
    rows = width // (NYL * NX * NC)
    block = NX * NC * rows
    part = block // 2
    source = lax.broadcasted_iota(jnp.int32, (block, block), 0)
    k = lax.broadcasted_iota(jnp.int32, (block, block), 1)
    second = (k >= part).astype(jnp.int32)
    k = k - part * second
    wanted = k + rows * (second + c - 2 * c * second)
    for b in range(1, NX):
        wanted = wanted + rows * (k >= b * rows).astype(jnp.int32)
    pick = (source == wanted).astype(F32).astype(BF)
    if norm:
        wide = value[...].astype(F32)
        r = lax.rsqrt(jnp.mean(wide * wide, axis=-1, keepdims=True) + 1e-06)
    for a in range(NYL):
        tokens = value[:, a * block : (a + 1) * block]
        if norm:
            tokens = (tokens.astype(F32) * r).astype(BF)
        moved = jnp.dot(tokens, pick, preferred_element_type=F32).astype(BF)
        own[:, a * part : (a + 1) * part] = moved[:, :part]
        away[:, a * part : (a + 1) * part] = moved[:, part:]


def prepare(value, norm):
    tokens, width = value.shape
    shape = jax.ShapeDtypeStruct((tokens, width // 2), BF)
    return pl.pallas_call(
        functools.partial(prepare_kernel, norm),
        out_shape=(shape, shape),
        in_specs=[VMEM],
        out_specs=(VMEM, VMEM),
        compiler_params=pltpu.CompilerParams(vmem_limit_bytes=LIMIT),
        name="prepare",
    )(value)


def project_kernel(blocks, own_l, own_c, arr_l, arr_c, mine, theirs, keep_l, keep_c, w):
    c = lax.axis_index("c")
    rows = blocks.shape[1]
    for yl, x, half, even, odd in half_shards():
        place = (yl * NX + x) * 2 + half
        w[place * rows : (place + 1) * rows] = blocks[jnp.where(c == 0, even, odd)]
    head = w.shape[1] // 4
    count = own_l.shape[0] // 2
    for frame, lat, cot in ((c, own_l, own_c), (1 - c, arr_l, arr_c)):
        for tokens, at in ((lat, slice(0, 3 * head)), (cot, slice(3 * head, 4 * head))):
            value = jnp.dot(tokens[...], w[:, at], preferred_element_type=F32)
            to = (mine.shape[0], mine.shape[2], at.stop - at.start)
            low, high = value[:count], value[count:]
            mine[:, frame, :, at] = jnp.where(c == 0, low, high).reshape(to)
            theirs[:, frame, :, at] = jnp.where(c == 0, high, low).reshape(to).astype(BF)
    keep_l[...] = arr_l[...]
    keep_c[...] = arr_c[...]


def project(blocks, own_l, own_c, arr_l, arr_c):
    tokens, width = own_l.shape
    columns = blocks.shape[-1]
    chips = NYL * NX
    shape = (chips, NC, tokens // (chips * NC), columns)
    kept = jax.ShapeDtypeStruct(arr_l.shape, BF)
    return pl.pallas_call(
        project_kernel,
        out_shape=(jax.ShapeDtypeStruct(shape, F32), jax.ShapeDtypeStruct(shape, BF), kept, kept),
        in_specs=[VMEM] * 5,
        out_specs=(VMEM,) * 4,
        scratch_shapes=[pltpu.VMEM((width, columns), BF)],
        compiler_params=pltpu.CompilerParams(vmem_limit_bytes=LIMIT),
        name="project",
    )(blocks, own_l, own_c, arr_l, arr_c)


def weight_kernel(back, own_l, arr_l, own_c, arr_c, blocks, grads):
    c = lax.axis_index("c")
    _, chips, _, patches, columns = back.shape
    head = columns // 4
    count = chips * patches
    rows = blocks.shape[1]
    for index, frame in ((0, c), (1, 1 - c)):
        for half in range(2):
            value = back[half, :, frame].astype(F32).reshape(count, columns)
            grads[index, half * count : (half + 1) * count] = value.astype(BF)
    wide = NX * 2 * rows

    def multiply(own, arrived, at, to):
        for yl in range(NYL):
            part = slice(yl * wide, (yl + 1) * wide)
            value = 0.0
            for index, tokens in ((0, own), (1, arrived)):
                value = value + lax.dot_general(
                    tokens[:, part],
                    grads[index, :, at],
                    (((0,), (0,)), ((), ())),
                    preferred_element_type=F32,
                )
            value = value.astype(BF)
            for y, x, half, even, odd in half_shards():
                if y == yl:
                    piece = value[(x * 2 + half) * rows : (x * 2 + half + 1) * rows]
                    blocks[jnp.where(c == 0, even, odd), :, to] = piece

    multiply(own_l, arr_l, slice(head, 4 * head), slice(0, 3 * head))
    multiply(own_c, arr_c, slice(0, head), slice(3 * head, 4 * head))


def weight_parts(back, own_l, own_c, arr_l, arr_c):
    tokens, width = own_l.shape
    columns = back.shape[-1]
    count = NYL * NX * 2
    return pl.pallas_call(
        weight_kernel,
        out_shape=jax.ShapeDtypeStruct((count, width // count, columns), BF),
        in_specs=[VMEM] * 5,
        out_specs=VMEM,
        scratch_shapes=[pltpu.VMEM((2, tokens, columns), BF)],
        compiler_params=pltpu.CompilerParams(vmem_limit_bytes=LIMIT),
        name="weight_parts",
    )(back, own_l, arr_l, own_c, arr_c)


def attend_kernel(packed, result):
    tokens, columns = packed.shape
    head = columns // 4
    scale = 1.0 / head**0.5
    patches = tokens // (NYL * NX * NC)
    query, keys, values, grad_out = (packed[:, i * head : (i + 1) * head] for i in range(4))
    row = lax.broadcasted_iota(jnp.int32, (tokens, tokens), 0)
    column = lax.broadcasted_iota(jnp.int32, (tokens, tokens), 1)
    same = lax.rem(row, patches) == lax.rem(column, patches)
    across, down = (((1,), (1,)), ((), ())), (((0,), (0,)), ((), ()))
    scores = lax.dot_general(query, keys, across, preferred_element_type=F32) * scale
    scores = jnp.where(same, scores, -jnp.inf)
    weights = jnp.exp(scores - jnp.max(scores, axis=-1, keepdims=True))
    probs = weights / jnp.sum(weights, axis=-1, keepdims=True)
    probs_b = probs.astype(BF)
    out = jnp.dot(probs_b, values, preferred_element_type=F32).astype(BF)
    result[:, :head] = out
    grad_v = lax.dot_general(probs_b, grad_out, down, preferred_element_type=F32)
    result[:, 3 * head :] = grad_v.astype(BF)
    grad_probs = lax.dot_general(grad_out, values, across, preferred_element_type=F32)
    delta = jnp.sum(grad_out.astype(F32) * out.astype(F32), axis=-1, keepdims=True)
    grad_scores = jnp.where(same, probs * (grad_probs - delta), 0.0).astype(BF)
    grad_q = jnp.dot(grad_scores, keys, preferred_element_type=F32) * scale
    result[:, head : 2 * head] = grad_q.astype(BF)
    grad_k = lax.dot_general(grad_scores, query, down, preferred_element_type=F32) * scale
    result[:, 2 * head : 3 * head] = grad_k.astype(BF)


def attend(packed):
    return pl.pallas_call(
        attend_kernel,
        out_shape=jax.ShapeDtypeStruct(packed.shape, BF),
        in_specs=[VMEM],
        out_specs=VMEM,
        compiler_params=pltpu.CompilerParams(vmem_limit_bytes=LIMIT),
        name="attend",
    )(packed)


def repeat_kernel(value, copies, sems):
    started = [pltpu.make_async_copy(value, copies.at[i], sems.at[i]) for i in range(copies.shape[0])]
    for copy in started:
        copy.start()
    for copy in started:
        copy.wait()


def repeat(value, count):
    return pl.pallas_call(
        repeat_kernel,
        out_shape=jax.ShapeDtypeStruct((count, *value.shape), value.dtype),
        in_specs=[VMEM],
        out_specs=HBM,
        scratch_shapes=[pltpu.SemaphoreType.DMA((count,))],
        compiler_params=pltpu.CompilerParams(vmem_limit_bytes=LIMIT),
        name="repeat",
    )(value)


def finish_kernel(copies, total):
    _, _, rows, columns = copies.shape
    for z1, z0 in itertools.product(range(NZ // 2), range(2)):
        index = z1 * 2 + z0
        value = copies[index, 0].astype(F32) + copies[index, 1].astype(F32)
        total[z0 * rows : (z0 + 1) * rows, z1 * columns : (z1 + 1) * columns] = value


def finish(copies):
    _, _, rows, columns = copies.shape
    return pl.pallas_call(
        finish_kernel,
        out_shape=jax.ShapeDtypeStruct((2 * rows, NZ // 2 * columns), F32),
        in_specs=[VMEM],
        out_specs=VMEM,
        compiler_params=pltpu.CompilerParams(vmem_limit_bytes=LIMIT),
        name="finish",
    )(copies)


def gather(weights, own):
    rows, columns = weights.shape
    z0 = lax.rem(lax.axis_index("z") + lax.axis_index("c"), 2)
    half = lax.dynamic_slice_in_dim(weights, z0 * (rows // 2), rows // 2)
    four = exchange(jnp.broadcast_to(half[None], (4, rows // 2, columns)), LIGHT)
    four, own = lax.optimization_barrier((four, own))
    blocks = exchange(repeat(four, 8), HEAVY)
    return blocks.reshape(32, rows // 2, columns), own


def reduce(blocks):
    _, rows, columns = blocks.shape
    heavy = exchange(blocks.reshape(8, 4, rows, columns), HEAVY)
    four = jnp.sum(heavy.astype(F32), axis=0).astype(BF)
    pieces = four.reshape(4, rows, 4, columns // 4).transpose(0, 2, 1, 3).reshape(16, rows, columns // 4)
    piece = jnp.sum(exchange(pieces, SPREAD).astype(F32), axis=0).astype(BF)
    copies = exchange(jnp.broadcast_to(piece[None], (NZ * NYH, *piece.shape)), COPIES)
    return finish(copies.reshape(NZ, NYH, *piece.shape))


def shards(latents, cotangent, weights):
    width = latents.shape[-1]
    columns = weights.shape[1]
    own_l, away_l = prepare(latents.reshape(-1, width), True)
    own_c, away_c = prepare(cotangent.reshape(-1, width), False)
    blocks, own_l = gather(weights, own_l)
    tokens = own_l, own_c, other_core(away_l), other_core(away_c)
    mine, theirs, *arrived = project(blocks, *tokens)
    tokens = *tokens[:2], *arrived
    both = lax.all_gather(theirs, "c")
    part = lax.dynamic_index_in_dim(both, 1 - lax.axis_index("c"), keepdims=False)
    packed = exchange((mine + part.astype(F32)).astype(BF), PLANE)
    result = attend(packed.reshape(-1, columns))
    back = lax.all_gather(exchange(result.reshape(packed.shape), PLANE), "c")
    return reduce(weight_parts(back, *tokens))


def solution(mesh):
    fine = Mesh(mesh.devices.reshape(NZ, NYH, NYL, NX, NC), AXES)
    dp, seq = ("z", "yh"), ("yl", "x", "c")
    placed = (P(dp, seq, None, None), P(dp, seq, None, None), P(seq, None))
    return jax.shard_map(shards, mesh=fine, in_specs=placed, out_specs=P(seq, None), check_vma=False)
```
